512 devices in a mesh: seq: 64 (over x, y, core), head: 8 (over z).
Axes of the slice: x: 4, y: 8, z: 8, core: 2. Of those that a mesh axis runs over, the one named last changes fastest.
Arguments:
- inner_x: bfloat16 [8192, 8192], P('seq', 'head'), may hold values from -6 to 6
- in_proj_b: bfloat16 [8192, 128], P('seq'), may hold values from -0.1796875 to 0.1796875
- in_proj_c: bfloat16 [8192, 128], P('seq'), may hold values from -0.1796875 to 0.1796875
- log_decay: float32 [128, 8192], P('head', 'seq'), may hold values from -1 to 0
- out_grad: bfloat16 [8192, 8192], P('seq', 'head'), may hold values from -6 to 6
Outputs:
- grad_inner_x: bfloat16 [8192, 8192], P('seq', 'head')
- grad_b: bfloat16 [8192, 128], P('seq')
- grad_c: bfloat16 [8192, 128], P('seq')
- grad_log_decay: float32 [128, 8192], P('head', 'seq')
The draws below stay inside these ranges and needn't reach their ends.
All inputs are finite; a program needn't handle non-finite values.
Results may differ from the reference program's by a relative error of at most 0.0057.
Values may be sent and summed in bfloat16 or wider, within the bound.
No kernel may reach another device: no remote copies, remote signals or barrier semaphores. Data moves between devices by JAX's collectives and lax.ppermute only.
A program may use at most 192 MiB of HBM per device.

```python
import math
import jax
import jax.numpy as jnp
from jax import lax

ATTENTION_GROUPS = 128
HEAD_DIM = 64
STATE = 128
TOK_DEV = 128
POSITION_COUNT = 8192
INNER = 8192
N_SEQ = 64


def draw_log_decay(key, part):
    key = jax.random.fold_in(key, 7)
    seed_for_variety, seed_for_gradual, seed_for_quick, seed_for_multiplier, seed_for_spike, seed_for_level = jax.random.split(key, 6)
    slow_share = 0.5
    is_slow = jax.random.uniform(seed_for_variety, (ATTENTION_GROUPS,)) < slow_share
    slow_rates = jnp.exp(jax.random.uniform(seed_for_gradual, (ATTENTION_GROUPS,), minval=math.log(0.1), maxval=math.log(0.5))) / POSITION_COUNT
    fast_rates = jnp.exp(jax.random.uniform(seed_for_quick, (ATTENTION_GROUPS,), minval=math.log(1.0 / 50.0), maxval=math.log(1.0 / 30.0)))
    forgetting_speeds = jnp.where(is_slow, slow_rates, fast_rates)
    multiplier_amplitude = jnp.exp(jax.random.uniform(seed_for_multiplier, (ATTENTION_GROUPS, POSITION_COUNT), minval=math.log(0.5), maxval=math.log(2.0)))
    spike_spans = jax.random.uniform(seed_for_spike, (ATTENTION_GROUPS, POSITION_COUNT)) < 2.0 / POSITION_COUNT
    stack_levels = jax.random.uniform(seed_for_level, (ATTENTION_GROUPS, POSITION_COUNT), minval=0.22, maxval=0.69)
    return (-(forgetting_speeds[:, None] * multiplier_amplitude) - jnp.where(spike_spans, stack_levels, 0.0)).astype(jnp.float32)


def shard_levels(own_key, extent, shards, smallest, high):
    loudness, own = 1.0, jax.random.fold_in(own_key, 6)
    for dim, parts in shards:
        heights = jnp.exp(jax.random.uniform(jax.random.fold_in(own, dim), (parts,), jnp.float32, smallest / len(shards), high / len(shards)))
        loudness = loudness * jnp.repeat(heights, extent[dim] // parts).reshape([-1 if axis == dim else 1 for axis in range(len(extent))])
    return loudness


def scatter_about(stream_key, dims, spread, reach, pieces=(), held_as=jnp.bfloat16):
    drawn = spread * jax.random.normal(stream_key, dims, jnp.float32)
    if pieces:
        drawn = drawn * shard_levels(stream_key, dims, pieces, -0.22, 0.18)
    return jnp.clip(drawn, -reach, reach).astype(held_as)


def setup_inputs(seed: int = 0) -> dict:
    key_list = jax.random.split(jax.random.key(seed), 6)
    inner_x = scatter_about(key_list[0], (POSITION_COUNT, INNER), 1.0, 6.0, ((0, 64), (1, 8)))
    in_proj_b = scatter_about(key_list[1], (POSITION_COUNT, STATE), 0.03, 0.1796875, ((0, 64),))
    in_proj_c = scatter_about(key_list[2], (POSITION_COUNT, STATE), 0.03, 0.1796875, ((0, 64),))
    log_decay = draw_log_decay(jax.random.fold_in(key_list[5], 71), 0)
    out_grad = scatter_about(key_list[4], (POSITION_COUNT, INNER), 1.0, 6.0, ((0, 64), (1, 8)))
    return {"inner_x": inner_x, "in_proj_b": in_proj_b, "in_proj_c": in_proj_c, "log_decay": log_decay, "out_grad": out_grad}


def combine(earlier, later):
    return (earlier[0] + later[0], jnp.exp(later[0])[:, None, None] * earlier[1] + later[1])


def head_step(running, inputs, b_mat, c_mat, b_float, c_float, scores, lower_mask):
    mixed_sum, b_cross, c_cross = running
    inner_h, grad_h, cumulative, total, entry, adjoint = inputs
    gaps = jnp.where(lower_mask, cumulative[:, None] - cumulative[None, :], 0.0)
    decays = jnp.where(lower_mask, jnp.exp(gaps), 0.0)
    kernel = (decays * scores).astype(jnp.bfloat16)
    to_end = jnp.exp(total - cumulative)
    from_start = jnp.exp(cumulative)
    adjoint_b = adjoint.astype(jnp.bfloat16)
    state_b = entry.astype(jnp.bfloat16)
    x_adjoint = jnp.dot(inner_h, adjoint_b, preferred_element_type=jnp.float32)
    grad_state = jnp.dot(grad_h, state_b, preferred_element_type=jnp.float32)
    b_adjoint = jnp.dot(b_mat, adjoint_b.T, preferred_element_type=jnp.float32)
    intra_grad = jnp.dot(kernel.T, grad_h, preferred_element_type=jnp.float32)
    grad_x = intra_grad + to_end[:, None] * b_adjoint
    pairs = jnp.dot(grad_h, inner_h.T, preferred_element_type=jnp.float32)
    mixed = decays * pairs
    weighted = mixed * scores
    colsum = jnp.sum(weighted, axis=0)
    rowsum = jnp.sum(weighted, axis=1)
    increments = colsum - jnp.concatenate([jnp.zeros((1,), jnp.float32), rowsum[:-1]])
    inner_q = jnp.cumsum(increments)
    alphas = from_start * jnp.sum(grad_state * c_float, axis=1)
    suffix = lax.cumsum(alphas, axis=0, reverse=True)
    betas = to_end * jnp.sum(x_adjoint * b_float, axis=1)
    prefix = jnp.cumsum(betas)
    constant = jnp.exp(total) * jnp.sum(adjoint * entry)
    decay_grad = inner_q + suffix + prefix + constant - jnp.sum(grad_x * inner_h.astype(jnp.float32), axis=1)
    updated = (mixed_sum + mixed, b_cross + to_end[:, None] * x_adjoint, c_cross + from_start[:, None] * grad_state)
    return updated, (grad_x.astype(jnp.bfloat16), decay_grad)


def prepare(block):
    inner_heads, grad_heads, b_mat, c_mat, decay_logs = block
    cumulative = jnp.cumsum(decay_logs, axis=1)
    totals = cumulative[:, -1]
    weighted_x = (inner_heads.astype(jnp.float32) * jnp.exp(totals[:, None] - cumulative)[:, :, None]).astype(jnp.bfloat16)
    weighted_grad = (grad_heads.astype(jnp.float32) * jnp.exp(cumulative)[:, :, None]).astype(jnp.bfloat16)
    end_states = jnp.einsum("htp,tn->hpn", weighted_x.astype(jnp.float32), b_mat.astype(jnp.float32))
    open_adjoints = jnp.einsum("htp,tn->hpn", weighted_grad.astype(jnp.float32), c_mat.astype(jnp.float32))
    return totals, end_states, open_adjoints


def block_grads(block):
    inner_heads, grad_heads, b_mat, c_mat, decay_logs, entries, adjoints = block
    cumulative = jnp.cumsum(decay_logs, axis=1)
    totals = cumulative[:, -1]
    b_float = b_mat.astype(jnp.float32)
    c_float = c_mat.astype(jnp.float32)
    scores = jnp.dot(c_mat, b_mat.T, preferred_element_type=jnp.float32)
    rows = lax.broadcasted_iota(jnp.int32, (TOK_DEV, TOK_DEV), 0)
    cols = lax.broadcasted_iota(jnp.int32, (TOK_DEV, TOK_DEV), 1)
    lower_mask = rows >= cols
    start = (jnp.zeros((TOK_DEV, TOK_DEV), jnp.float32), jnp.zeros((TOK_DEV, STATE), jnp.float32), jnp.zeros((TOK_DEV, STATE), jnp.float32))

    def scan_head(running, inputs):
        return head_step(running, inputs, b_mat, c_mat, b_float, c_float, scores, lower_mask)

    sums, outs = lax.scan(scan_head, start, (inner_heads, grad_heads, cumulative, totals, entries, adjoints))
    mixed_sum, b_cross, c_cross = sums
    b_sum = jnp.dot(mixed_sum.T, c_float, precision=lax.Precision.HIGHEST) + b_cross
    c_sum = jnp.dot(mixed_sum, b_float, precision=lax.Precision.HIGHEST) + c_cross
    return outs[0], outs[1], b_sum, c_sum


def reference(inner_x, in_proj_b, in_proj_c, log_decay, out_grad):
    inner_blocks = inner_x.reshape(N_SEQ, TOK_DEV, ATTENTION_GROUPS, HEAD_DIM).transpose(0, 2, 1, 3)
    grad_blocks = out_grad.reshape(N_SEQ, TOK_DEV, ATTENTION_GROUPS, HEAD_DIM).transpose(0, 2, 1, 3)
    b_blocks = in_proj_b.reshape(N_SEQ, TOK_DEV, STATE)
    c_blocks = in_proj_c.reshape(N_SEQ, TOK_DEV, STATE)
    decay_blocks = log_decay.reshape(ATTENTION_GROUPS, N_SEQ, TOK_DEV).transpose(1, 0, 2)
    totals, end_states, open_adjoints = lax.map(prepare, (inner_blocks, grad_blocks, b_blocks, c_blocks, decay_blocks))
    initial = (jnp.zeros((ATTENTION_GROUPS,), jnp.float32), jnp.zeros((ATTENTION_GROUPS, HEAD_DIM, STATE), jnp.float32))

    def chain_step(running, element):
        return combine(running, element), running[1]

    unused_f, entries = lax.scan(chain_step, initial, (totals, end_states))
    unused_r, adjoints = lax.scan(chain_step, initial, (totals, open_adjoints), reverse=True)
    grad_x, decay_grad, b_sum, c_sum = lax.map(block_grads, (inner_blocks, grad_blocks, b_blocks, c_blocks, decay_blocks, entries, adjoints))
    grad_inner_x = grad_x.transpose(0, 2, 1, 3).reshape(POSITION_COUNT, INNER)
    grad_log_decay = decay_grad.transpose(1, 0, 2).reshape(ATTENTION_GROUPS, POSITION_COUNT)
    grad_b = b_sum.reshape(POSITION_COUNT, STATE).astype(jnp.bfloat16)
    grad_c = c_sum.reshape(POSITION_COUNT, STATE).astype(jnp.bfloat16)
    return grad_inner_x, grad_b, grad_c, grad_log_decay
```

```python
import functools

import jax
import jax.numpy as jnp
from jax import lax
from jax.experimental import pallas as pl
from jax.experimental.pallas import tpu as pltpu
from jax.sharding import PartitionSpec as P

F32 = jnp.float32
BF16 = jnp.bfloat16
HIGHEST = lax.Precision.HIGHEST
TOK = 128
LANES = 128
HALF = 64
HEADS = 16
PAIRS = 8
ROWS = 16
SEND_ROWS = 40


def nn(a, b, precision=None):
    return lax.dot_general(
        a, b, (((1,), (0,)), ((), ())), precision=precision, preferred_element_type=F32
    )


def nt(a, b, precision=None):
    return lax.dot_general(
        a, b, (((1,), (1,)), ((), ())), precision=precision, preferred_element_type=F32
    )


def iota(dim, shape=(TOK, LANES)):
    return lax.broadcasted_iota(jnp.int32, shape, dim)


def pair(g):
    return slice(g * LANES, (g + 1) * LANES)


def transposed(matrix):
    return matrix.astype(F32).T.astype(BF16)


def cumulative_columns(log_decay):
    lower = (iota(0) >= iota(1)).astype(F32)
    return nt(lower, log_decay, HIGHEST)


def spread(columns, g):
    rows = columns.shape[0]
    left = iota(1, (rows, LANES)) < HALF
    a = jnp.broadcast_to(columns[:, 2 * g : 2 * g + 1], (rows, LANES))
    b = jnp.broadcast_to(columns[:, 2 * g + 1 : 2 * g + 2], (rows, LANES))
    return jnp.where(left, a, b)


def states_kernel(x_ref, b_ref, c_ref, log_ref, grad_ref, send_ref, wx_ref, wg_ref):
    cum = cumulative_columns(log_ref[...])
    total = cum[TOK - 1 : TOK, :]
    to_end = jnp.exp(total - cum)
    from_start = jnp.exp(cum)
    b_t = transposed(b_ref[...])
    c_t = transposed(c_ref[...])
    for g in range(PAIRS):
        spread_start = spread(from_start, g)
        wx = (x_ref[:, pair(g)].astype(F32) * spread(to_end, g)).astype(BF16)
        wg = (grad_ref[:, pair(g)].astype(F32) * spread_start).astype(BF16)
        wx_ref[:, pair(g)] = wx
        wg_ref[:, pair(g)] = wg
        ends = nn(b_t, wx).astype(BF16)
        opens = nn(c_t, wg).astype(BF16)
        factor = jnp.broadcast_to(spread_start[TOK - 1 : TOK, :], (8, LANES))
        high = factor.astype(BF16).astype(F32)
        first = iota(0, (8, LANES)) == 0
        factors = jnp.where(first, high, factor - high).astype(BF16)
        for r in range(PAIRS):
            rows = slice(r * ROWS, (r + 1) * ROWS)
            send_ref[g * PAIRS + r] = jnp.concatenate([ends[rows], opens[rows], factors], axis=0)


def recurrence_kernel(got_ref, back_ref):
    count = got_ref.shape[0]

    def factor(k):
        parts = got_ref[k, 2 * ROWS : SEND_ROWS, :].astype(F32)
        return parts[0:1, :] + parts[1:2, :]

    entry = jnp.zeros((ROWS, LANES), F32)
    adjoint = jnp.zeros((ROWS, LANES), F32)
    for k in range(count):
        back_ref[k, 0:ROWS, :] = entry.astype(BF16)
        entry = factor(k) * entry + got_ref[k, 0:ROWS, :].astype(F32)
        m = count - 1 - k
        back_ref[m, ROWS : 2 * ROWS, :] = adjoint.astype(BF16)
        adjoint = factor(m) * adjoint + got_ref[m, ROWS : 2 * ROWS, :].astype(F32)


def intra_kernel(x_ref, b_ref, c_ref, log_ref, grad_ref, gx_ref, decay_ref, bc_ref):
    log_decay = log_ref[...]
    upper = (iota(0) <= iota(1)).astype(F32)
    cum_rows = nn(log_decay, upper, HIGHEST)
    cum = cumulative_columns(log_decay)
    b_mat = b_ref[...]
    c_mat = c_ref[...]
    scores = nt(b_mat, c_mat)
    later = iota(1) >= iota(0)
    before = iota(0) < iota(1)
    ends_after = (iota(0) >= iota(1)).astype(BF16)
    left = iota(1) < HALF
    mixed_sum = jnp.zeros((TOK, TOK), F32)
    for g in range(PAIRS):
        x_g = x_ref[:, pair(g)]
        grad_g = grad_ref[:, pair(g)]
        grad_x = jnp.zeros((TOK, LANES), F32)
        for j in range(2):
            h = 2 * g + j
            mine = left if j == 0 else jnp.logical_not(left)
            x_h = jnp.where(mine, x_g, jnp.zeros_like(x_g))
            grad_h = jnp.where(mine, grad_g, jnp.zeros_like(grad_g))
            pairs = nt(x_h, grad_g)
            gaps = cum_rows[h : h + 1, :] - cum[:, h : h + 1]
            decays = jnp.exp(jnp.where(later, gaps, -1e4))
            kernel = decays * scores
            mixed_sum = mixed_sum + decays * pairs
            grad_x = grad_x + nn(kernel.astype(BF16), grad_h)
            weighted = (kernel * pairs).astype(BF16)
            reach = nn(weighted, ends_after)
            decay_ref[h : h + 1, :] = jnp.sum(
                jnp.where(before, reach, 0.0), axis=0, keepdims=True
            )
        gx_ref[:, pair(g)] = grad_x
    high = mixed_sum.astype(BF16)
    low = (mixed_sum - high.astype(F32)).astype(BF16)
    mixed_t = mixed_sum.T
    high_t = mixed_t.astype(BF16)
    low_t = (mixed_t - high_t.astype(F32)).astype(BF16)
    bc_ref[0:TOK, :] = nn(high, c_mat) + nn(low, c_mat)
    bc_ref[TOK : 2 * TOK, :] = nn(high_t, b_mat) + nn(low_t, b_mat)


def cross_kernel(
    back_ref, x_ref, b_ref, c_ref, log_ref, grad_ref, wx_ref, wg_ref, gx_ref, inner_ref, bc_ref,
    out_ref, decay_ref, send_ref,
):
    cum = cumulative_columns(log_ref[...])
    total = cum[TOK - 1 : TOK, :]
    to_end = jnp.exp(total - cum)
    from_start = jnp.exp(cum)
    b_mat = b_ref[...]
    c_mat = c_ref[...]
    b_sum = bc_ref[0:TOK, :]
    c_sum = bc_ref[TOK : 2 * TOK, :]
    last = iota(0) == TOK - 1
    alphas = jnp.zeros((HEADS, TOK), F32)
    betas = jnp.zeros((HEADS, TOK), F32)
    for g in range(PAIRS):
        entry = back_ref[g * PAIRS : (g + 1) * PAIRS, 0:ROWS, :].reshape(TOK, LANES)
        adjoint = back_ref[g * PAIRS : (g + 1) * PAIRS, ROWS : 2 * ROWS, :].reshape(TOK, LANES)
        start_g = spread(from_start, g)
        cross = spread(to_end, g) * nn(b_mat, adjoint)
        out_ref[:, pair(g)] = (gx_ref[:, pair(g)] + cross).astype(BF16)
        beta = x_ref[:, pair(g)].astype(F32) * cross
        alpha = grad_ref[:, pair(g)].astype(F32) * (start_g * nn(c_mat, entry))
        overlap = jnp.sum(entry.astype(F32) * adjoint.astype(F32), axis=0, keepdims=True)
        alpha = alpha + jnp.where(last, start_g * overlap, 0.0)
        head_of = 2 * g + iota(1, (HEADS, LANES)) // HALF
        pick = (iota(0, (HEADS, LANES)) == head_of).astype(BF16)
        beta_high = beta.astype(BF16)
        alpha_high = alpha.astype(BF16)
        betas = betas + nt(pick, beta_high) + nt(pick, (beta - beta_high.astype(F32)).astype(BF16))
        alphas = (
            alphas + nt(pick, alpha_high) + nt(pick, (alpha - alpha_high.astype(F32)).astype(BF16))
        )
        b_sum = b_sum + nt(wx_ref[:, pair(g)], adjoint)
        c_sum = c_sum + nt(wg_ref[:, pair(g)], entry)
    before = (iota(0) < iota(1)).astype(F32)
    after = (iota(0) >= iota(1)).astype(F32)
    decay_ref[...] = inner_ref[...] + nn(betas, before, HIGHEST) + nn(alphas, after, HIGHEST)
    b_out = b_sum.astype(BF16)
    c_out = c_sum.astype(BF16)
    for z in range(send_ref.shape[0]):
        send_ref[z, 0:TOK, :] = b_out
        send_ref[z, TOK : 2 * TOK, :] = c_out


def call(body, outs, flops, *args):
    return pl.pallas_call(
        body,
        out_shape=[jax.ShapeDtypeStruct(s, d) for s, d in outs],
        compiler_params=pltpu.CompilerParams(vmem_limit_bytes=32 * 1024 * 1024),
        cost_estimate=pl.CostEstimate(flops=flops, bytes_accessed=2 << 20, transcendentals=0),
    )(*args)


def per_device(seq, heads, x, b_mat, c_mat, log_decay, grad):
    wide = (TOK, HEADS * HALF)
    send, wx, wg = call(
        states_kernel,
        [((seq, SEND_ROWS, LANES), BF16), (wide, BF16), (wide, BF16)],
        1 << 27,
        x, b_mat, c_mat, log_decay, grad,
    )
    got = lax.all_to_all(send, "seq", 0, 0, tiled=True)
    gx, inner, bc = call(
        intra_kernel,
        [(wide, F32), ((HEADS, TOK), F32), ((2 * TOK, LANES), F32)],
        1 << 29,
        x, b_mat, c_mat, log_decay, grad,
    )
    (back,) = call(recurrence_kernel, [((seq, 2 * ROWS, LANES), BF16)], 1 << 20, got)
    back = lax.all_to_all(back, "seq", 0, 0, tiled=True)
    grad_x, decay_grad, parts = call(
        cross_kernel,
        [(wide, BF16), ((HEADS, TOK), F32), ((heads, 2 * TOK, LANES), BF16)],
        1 << 28,
        back, x, b_mat, c_mat, log_decay, grad, wx, wg, gx, inner, bc,
    )
    parts = lax.all_to_all(parts, "head", 0, 0, tiled=True)
    sums = jnp.sum(parts.astype(F32), axis=0).astype(BF16)
    return grad_x, sums[:TOK], sums[TOK:], decay_grad


def solution(mesh):
    in_specs = (
        P("seq", "head"),
        P("seq", None),
        P("seq", None),
        P("head", "seq"),
        P("seq", "head"),
    )
    out_specs = (P("seq", "head"), P("seq", None), P("seq", None), P("head", "seq"))
    return jax.shard_map(
        functools.partial(per_device, mesh.shape["seq"], mesh.shape["head"]),
        mesh=mesh,
        in_specs=in_specs,
        out_specs=out_specs,
        check_vma=False,
    )
```

```python
import functools

import jax
import jax.numpy as jnp
from jax import lax
from jax.experimental import pallas as pl
from jax.experimental.pallas import tpu as pltpu
from jax.sharding import PartitionSpec as P

F32 = jnp.float32
BF16 = jnp.bfloat16
HIGHEST = lax.Precision.HIGHEST
TOK = 128
LANES = 128
HALF = 64
HEADS = 16
WIDE = HEADS * HALF
PAIRS = 8
CHUNKS = 8
ROWS = 16
SEND_ROWS = 2 * ROWS + 8
TAIL = 16


def nn(a, b, precision=None):
    return lax.dot_general(
        a, b, (((1,), (0,)), ((), ())), precision=precision, preferred_element_type=F32
    )


def nt(a, b, precision=None):
    return lax.dot_general(
        a, b, (((1,), (1,)), ((), ())), precision=precision, preferred_element_type=F32
    )


def iota(dim, shape=(TOK, LANES)):
    return lax.broadcasted_iota(jnp.int32, shape, dim)


def pair(g):
    return slice(g * LANES, (g + 1) * LANES)


def transposed(matrix):
    return matrix.astype(F32).T.astype(BF16)


def split(value):
    high = value.astype(BF16)
    return high, (value - high.astype(F32)).astype(BF16)


def cumulative_columns(log_decay):
    lower = (iota(0) >= iota(1)).astype(F32)
    return nt(lower, log_decay, HIGHEST)


def spread(columns, g):
    rows = columns.shape[0]
    left = iota(1, (rows, LANES)) < HALF
    a = jnp.broadcast_to(columns[:, 2 * g : 2 * g + 1], (rows, LANES))
    b = jnp.broadcast_to(columns[:, 2 * g + 1 : 2 * g + 2], (rows, LANES))
    return jnp.where(left, a, b)


def core():
    return lax.axis_index("seq") % 2


def first_core(shape):
    return jnp.full(shape, core(), jnp.int32) == 0


def half_pair(half, i):
    return pl.ds(pl.multiple_of(half * (WIDE // 2) + i * LANES, LANES), LANES)


def two_rows(value, rows):
    wide = jnp.broadcast_to(value, (rows, LANES))
    high = wide.astype(BF16).astype(F32)
    return jnp.where(iota(0, (rows, LANES)) == 0, high, wide - high).astype(BF16)


def one_row(rows):
    rows = rows.astype(F32)
    return rows[0:1, :] + rows[1:2, :]


def load(pairs, sems):
    copies = [pltpu.make_async_copy(a, b, sems.at[i]) for i, (a, b) in enumerate(pairs)]
    for copy in copies:
        copy.start()
    return copies


def states_kernel(
    x_hbm, b_hbm, c_hbm, log_hbm, grad_hbm,
    send_ref, mine_ref, factor_ref,
    x_ref, b_ref, c_ref, log_ref, grad_ref, sems,
):
    copies = load(
        [(log_hbm, log_ref), (b_hbm, b_ref), (c_hbm, c_ref), (x_hbm, x_ref), (grad_hbm, grad_ref)],
        sems,
    )
    copies[0].wait()
    cum = cumulative_columns(log_ref[...])
    total = cum[TOK - 1 : TOK, :]
    to_end = jnp.exp(total - cum)
    from_start = jnp.exp(cum)
    last = jnp.exp(total)
    copies[1].wait()
    b_t = transposed(b_ref[...])
    copies[2].wait()
    c_t = transposed(c_ref[...])
    copies[3].wait()
    copies[4].wait()
    for g in range(PAIRS):
        wx = (x_ref[:, pair(g)].astype(F32) * spread(to_end, g)).astype(BF16)
        wg = (grad_ref[:, pair(g)].astype(F32) * spread(from_start, g)).astype(BF16)
        ends = nn(b_t, wx)
        opens = nn(c_t, wg)
        factor = spread(last, g)
        mine_ref[0:TOK, pair(g)] = ends
        mine_ref[TOK : 2 * TOK, pair(g)] = opens
        send_ref[0:TOK, pair(g)] = ends.astype(BF16)
        send_ref[TOK : 2 * TOK, pair(g)] = opens.astype(BF16)
        send_ref[2 * TOK : 2 * TOK + TAIL, pair(g)] = two_rows(factor, TAIL)
        factor_ref[:, pair(g)] = jnp.broadcast_to(factor, (8, LANES))


def chip_kernel(got_ref, mine_ref, factor_ref, send_ref):
    half = core()
    first = first_core((TOK, LANES))
    first_row = first_core((1, LANES))
    for i in range(PAIRS // 2):
        lanes = half_pair(half, i)
        mine = factor_ref[0:1, lanes]
        theirs = one_row(got_ref[2 * TOK : 2 * TOK + TAIL, lanes])
        factor0 = jnp.where(first_row, mine, theirs)
        factor1 = jnp.where(first_row, theirs, mine)
        my_ends = mine_ref[0:TOK, lanes]
        my_opens = mine_ref[TOK : 2 * TOK, lanes]
        ends = got_ref[0:TOK, lanes].astype(F32)
        opens = got_ref[TOK : 2 * TOK, lanes].astype(F32)
        chip_ends = factor1 * jnp.where(first, my_ends, ends) + jnp.where(first, ends, my_ends)
        chip_opens = factor0 * jnp.where(first, opens, my_opens) + jnp.where(first, my_opens, opens)
        chip_ends = chip_ends.astype(BF16)
        chip_opens = chip_opens.astype(BF16)
        factors = two_rows(mine * theirs, 8)
        for r in range(CHUNKS):
            rows = slice(r * ROWS, (r + 1) * ROWS)
            send_ref[i * CHUNKS + r] = jnp.concatenate(
                [chip_ends[rows], chip_opens[rows], factors], axis=0
            )


def recurrence_kernel(got_ref, back_ref):
    count = got_ref.shape[0]
    entry = jnp.zeros((ROWS, LANES), F32)
    adjoint = jnp.zeros((ROWS, LANES), F32)
    entries, adjoints = [None] * count, [None] * count
    for k in range(count):
        m = count - 1 - k
        entries[k], adjoints[m] = entry, adjoint
        entry = one_row(got_ref[k, 2 * ROWS : SEND_ROWS]) * entry + got_ref[k, 0:ROWS].astype(F32)
        adjoint = one_row(got_ref[m, 2 * ROWS : SEND_ROWS]) * adjoint + got_ref[
            m, ROWS : 2 * ROWS
        ].astype(F32)
    for k in range(count):
        overlap = jnp.sum(entries[k] * adjoints[k], axis=0, keepdims=True)
        back_ref[k] = jnp.concatenate(
            [entries[k].astype(BF16), adjoints[k].astype(BF16), two_rows(overlap, 8)], axis=0
        )


def intra_kernel(
    x_hbm, b_hbm, c_hbm, log_hbm, grad_hbm,
    gx_ref, decay_ref, bc_ref, wx_ref, wg_ref, mats_ref, end_ref,
    x_ref, b_ref, c_ref, log_ref, grad_ref, sems,
):
    copies = load(
        [(log_hbm, log_ref), (b_hbm, b_ref), (c_hbm, c_ref), (x_hbm, x_ref), (grad_hbm, grad_ref)],
        sems,
    )
    for copy in copies:
        copy.wait()
    log_decay = log_ref[...]
    upper = (iota(0) <= iota(1)).astype(F32)
    cum_rows = nn(log_decay, upper, HIGHEST)
    cum = cumulative_columns(log_decay)
    to_end = jnp.exp(cum[TOK - 1 : TOK, :] - cum)
    from_start = jnp.exp(cum)
    b_mat = b_ref[...]
    c_mat = c_ref[...]
    mats_ref[0] = b_mat
    mats_ref[1] = c_mat
    scores = nt(b_mat, c_mat)
    later = iota(1) >= iota(0)
    before = iota(0) < iota(1)
    ends_after = (iota(0) >= iota(1)).astype(BF16)
    left = iota(1) < HALF
    mixed_sum = jnp.zeros((TOK, TOK), F32)
    for g in range(PAIRS):
        x_g = x_ref[:, pair(g)]
        grad_g = grad_ref[:, pair(g)]
        end_g = spread(to_end, g)
        end_ref[:, pair(g)] = end_g
        wx_ref[:, pair(g)] = (x_g.astype(F32) * end_g).astype(BF16)
        wg_ref[:, pair(g)] = (grad_g.astype(F32) * spread(from_start, g)).astype(BF16)
        grad_x = jnp.zeros((TOK, LANES), F32)
        for j in range(2):
            h = 2 * g + j
            mine = left if j == 0 else jnp.logical_not(left)
            x_h = jnp.where(mine, x_g, jnp.zeros_like(x_g))
            grad_h = jnp.where(mine, grad_g, jnp.zeros_like(grad_g))
            pairs = nt(x_h, grad_g)
            gaps = cum_rows[h : h + 1, :] - cum[:, h : h + 1]
            decays = jnp.exp(jnp.where(later, gaps, -1e4))
            kernel = decays * scores
            mixed_sum = mixed_sum + decays * pairs
            grad_x = grad_x + nn(kernel.astype(BF16), grad_h)
            reach = nn((kernel * pairs).astype(BF16), ends_after)
            decay_ref[h : h + 1, :] = jnp.sum(
                jnp.where(before, reach, 0.0), axis=0, keepdims=True
            )
        gx_ref[:, pair(g)] = grad_x
    high, low = split(mixed_sum)
    high_t, low_t = split(mixed_sum.T)
    bc_ref[0] = nn(high, c_mat) + nn(low, c_mat)
    bc_ref[1] = nn(high_t, b_mat) + nn(low_t, b_mat)


def slices(ref, i, start, rows):
    return ref[i * CHUNKS : (i + 1) * CHUNKS, start : start + rows, :]


def half_sums(half, back_ref, got_ref, wx_ref, wg_ref, b_sum, c_sum, state_ref):
    first = first_core((TOK, LANES))
    for i in range(PAIRS // 2):
        lanes = half_pair(half, i)
        theirs = one_row(got_ref[2 * TOK : 2 * TOK + TAIL, lanes])
        entry = slices(back_ref, i, 0, ROWS).reshape(TOK, LANES)
        adjoint = slices(back_ref, i, ROWS, ROWS).reshape(TOK, LANES)
        inside = jnp.where(first, adjoint.astype(F32), entry.astype(F32)) * theirs
        added = jnp.where(
            first, got_ref[TOK : 2 * TOK, lanes].astype(F32), got_ref[0:TOK, lanes].astype(F32)
        )
        inside = inside + added
        entry = jnp.where(first, entry.astype(F32), inside).astype(BF16)
        adjoint = jnp.where(first, inside, adjoint.astype(F32)).astype(BF16)
        state_ref[0, :, i * LANES : (i + 1) * LANES] = entry
        state_ref[1, :, i * LANES : (i + 1) * LANES] = adjoint
        b_sum = b_sum + nt(wx_ref[:, lanes], adjoint)
        c_sum = c_sum + nt(wg_ref[:, lanes], entry)
    return b_sum, c_sum


def own_kernel(back_ref, got_ref, wx_ref, wg_ref, bc_ref, state_ref, part_ref):
    part_ref[0], part_ref[1] = half_sums(
        core(), back_ref, got_ref, wx_ref, wg_ref, bc_ref[0], bc_ref[1], state_ref
    )


def other_kernel(back_ref, got_ref, wx_ref, wg_ref, part_ref, state_ref, send_ref):
    b_sum, c_sum = half_sums(
        1 - core(), back_ref, got_ref, wx_ref, wg_ref, part_ref[0], part_ref[1], state_ref
    )
    b_out = b_sum.astype(BF16)
    c_out = c_sum.astype(BF16)
    for z in range(send_ref.shape[0]):
        send_ref[z, 0:TOK, :] = b_out
        send_ref[z, TOK : 2 * TOK, :] = c_out


def grads_kernel(
    own_ref, other_ref, own_state_ref, other_state_ref, got_ref, factor_ref,
    wx_ref, wg_ref, mats_ref, gx_ref, inner_ref, end_ref,
    out_ref, decay_ref,
):
    first = first_core((TOK, LANES))
    b_mat = mats_ref[0]
    c_mat = mats_ref[1]
    last = iota(0) == TOK - 1
    alphas = jnp.zeros((TOK, LANES), F32)
    betas = jnp.zeros((TOK, LANES), F32)
    for half, back_ref, state_ref in (
        (core(), own_ref, own_state_ref),
        (1 - core(), other_ref, other_state_ref),
    ):
        for i in range(PAIRS // 2):
            lanes = half_pair(half, i)
            entry = state_ref[0, :, i * LANES : (i + 1) * LANES]
            adjoint = state_ref[1, :, i * LANES : (i + 1) * LANES]
            from_adjoint = nn(b_mat, adjoint)
            out_ref[:, lanes] = (gx_ref[:, lanes] + end_ref[:, lanes] * from_adjoint).astype(BF16)
            beta = wx_ref[:, lanes].astype(F32) * from_adjoint
            alpha = wg_ref[:, lanes].astype(F32) * nn(c_mat, entry)
            chip = one_row(jnp.sum(slices(back_ref, i, 2 * ROWS, 8).astype(F32), axis=0))
            outer = jnp.where(
                first,
                slices(back_ref, i, 0, ROWS).reshape(TOK, LANES).astype(F32)
                * got_ref[TOK : 2 * TOK, lanes].astype(F32),
                slices(back_ref, i, ROWS, ROWS).reshape(TOK, LANES).astype(F32)
                * got_ref[0:TOK, lanes].astype(F32),
            )
            theirs = one_row(got_ref[2 * TOK : 2 * TOK + TAIL, lanes])
            constant = factor_ref[0:1, lanes] * (
                theirs * chip + jnp.sum(outer, axis=0, keepdims=True)
            )
            alpha = alpha + jnp.where(last, constant, 0.0)
            head = 2 * (half * (PAIRS // 2) + i)
            pick = (iota(1) == head + iota(0) // HALF).astype(BF16)
            beta_high, beta_low = split(beta)
            alpha_high, alpha_low = split(alpha)
            betas = betas + nn(beta_high, pick) + nn(beta_low, pick)
            alphas = alphas + nn(alpha_high, pick) + nn(alpha_low, pick)
    after = (iota(0) <= iota(1)).astype(F32)
    before = (iota(0) > iota(1)).astype(F32)
    decay = nn(after, alphas, HIGHEST) + nn(before, betas, HIGHEST)
    decay_ref[...] = inner_ref[...] + decay.T[0:HEADS, :]


def head_sum_kernel(parts_ref, b_ref, c_ref):
    b_ref[...] = jnp.sum(parts_ref[:, 0:TOK, :].astype(F32), axis=0).astype(BF16)
    c_ref[...] = jnp.sum(parts_ref[:, TOK : 2 * TOK, :].astype(F32), axis=0).astype(BF16)


HBM_SPEC = pl.BlockSpec(memory_space=pltpu.HBM)


def call(body, outs, micros, *args, from_hbm=False, scratch=()):
    more = {}
    if from_hbm:
        more["in_specs"] = [HBM_SPEC] * len(args)
        args = [pltpu.with_memory_space_constraint(a, pltpu.HBM) for a in args]
    return pl.pallas_call(
        body,
        out_shape=[jax.ShapeDtypeStruct(s, d) for s, d in outs],
        scratch_shapes=list(scratch),
        compiler_params=pltpu.CompilerParams(vmem_limit_bytes=24 * 1024 * 1024),
        cost_estimate=pl.CostEstimate(
            flops=int(micros * 1e9), bytes_accessed=1 << 18, transcendentals=0
        ),
        **more,
    )(*args)


def per_device(seq, heads, x, b_mat, c_mat, log_decay, grad):
    chips = seq // 2
    assert chips == PAIRS // 2 * CHUNKS
    inputs = (x, b_mat, c_mat, log_decay, grad)
    swap = [(i, i ^ 1) for i in range(seq)]
    same_core = [[2 * m + c for m in range(chips)] for c in range(2)]
    wide = (TOK, WIDE)
    half_state = ((2, TOK, WIDE // 2), BF16)
    loaded = (
        pltpu.VMEM(wide, BF16),
        pltpu.VMEM((TOK, LANES), BF16),
        pltpu.VMEM((TOK, LANES), BF16),
        pltpu.VMEM((HEADS, TOK), F32),
        pltpu.VMEM(wide, BF16),
        pltpu.SemaphoreType.DMA((5,)),
    )
    send, mine, factor = call(
        states_kernel,
        [((2 * TOK + TAIL, WIDE), BF16), ((2 * TOK, WIDE), F32), ((8, WIDE), F32)],
        1,
        *inputs,
        from_hbm=True,
        scratch=loaded,
    )
    got = lax.ppermute(send, "seq", swap)
    (send,) = call(chip_kernel, [((chips, SEND_ROWS, LANES), BF16)], 1, got, mine, factor)
    gathered = lax.all_to_all(send, "seq", 0, 0, tiled=True, axis_index_groups=same_core)
    local = call(
        intra_kernel,
        [
            (wide, F32),
            ((HEADS, TOK), F32),
            ((2, TOK, LANES), F32),
            (wide, BF16),
            (wide, BF16),
            ((2, TOK, LANES), BF16),
            (wide, F32),
        ],
        3,
        *inputs,
        from_hbm=True,
        scratch=loaded,
    )
    gathered, (gx, inner, bc, wx, wg, mats, end) = lax.optimization_barrier((gathered, local))
    (back,) = call(recurrence_kernel, [((chips, SEND_ROWS, LANES), BF16)], 1, gathered)
    back = lax.all_to_all(back, "seq", 0, 0, tiled=True, axis_index_groups=same_core)
    other = lax.ppermute(back, "seq", swap)
    own_state, part = call(
        own_kernel, [half_state, ((2, TOK, LANES), F32)], 1, back, got, wx, wg, bc
    )
    other_state, parts = call(
        other_kernel,
        [half_state, ((heads, 2 * TOK, LANES), BF16)],
        1, other, got, wx, wg, part,
    )
    parts = lax.all_to_all(parts, "head", 0, 0, tiled=True)
    grad_x, decay_grad = call(
        grads_kernel,
        [(wide, BF16), ((HEADS, TOK), F32)],
        3,
        back, other, own_state, other_state, got, factor, wx, wg, mats, gx, inner, end,
    )
    parts, grad_x, decay_grad = lax.optimization_barrier((parts, grad_x, decay_grad))
    grad_b, grad_c = call(head_sum_kernel, [((TOK, LANES), BF16)] * 2, 1, parts)
    return grad_x, grad_b, grad_c, decay_grad


def solution(mesh):
    in_specs = (
        P("seq", "head"),
        P("seq", None),
        P("seq", None),
        P("head", "seq"),
        P("seq", "head"),
    )
    out_specs = (P("seq", "head"), P("seq", None), P("seq", None), P("head", "seq"))
    return jax.shard_map(
        functools.partial(per_device, mesh.shape["seq"], mesh.shape["head"]),
        mesh=mesh,
        in_specs=in_specs,
        out_specs=out_specs,
        check_vma=False,
    )
```

```python
import functools

import jax
import jax.numpy as jnp
from jax import lax
from jax.experimental import pallas as pl
from jax.experimental.pallas import tpu as pltpu
from jax.sharding import PartitionSpec as P

F32 = jnp.float32
BF16 = jnp.bfloat16
HIGHEST = lax.Precision.HIGHEST
TOK = 128
LANES = 128
HALF = 64
HEADS = 16
WIDE = HEADS * HALF
HALF_WIDE = WIDE // 2
PAIRS = 8
CHUNKS = 8
ROWS = 16
SEND_ROWS = 2 * ROWS + 8
TAIL = 16


def nn(a, b, precision=None):
    return lax.dot_general(
        a, b, (((1,), (0,)), ((), ())), precision=precision, preferred_element_type=F32
    )


def nt(a, b, precision=None):
    return lax.dot_general(
        a, b, (((1,), (1,)), ((), ())), precision=precision, preferred_element_type=F32
    )


def iota(dim, shape=(TOK, LANES)):
    return lax.broadcasted_iota(jnp.int32, shape, dim)


def pair(g):
    return slice(g * LANES, (g + 1) * LANES)


def transposed(matrix):
    return matrix.astype(F32).T.astype(BF16)


def split(value):
    high = value.astype(BF16)
    return high, (value - high.astype(F32)).astype(BF16)


def cumulative_columns(log_decay):
    lower = (iota(0) >= iota(1)).astype(F32)
    return nt(lower, log_decay, HIGHEST)


def spread(columns, g):
    rows = columns.shape[0]
    left = iota(1, (rows, LANES)) < HALF
    a = jnp.broadcast_to(columns[:, 2 * g : 2 * g + 1], (rows, LANES))
    b = jnp.broadcast_to(columns[:, 2 * g + 1 : 2 * g + 2], (rows, LANES))
    return jnp.where(left, a, b)


def core():
    return lax.axis_index("seq") % 2


def first_core(shape):
    return jnp.full(shape, core(), jnp.int32) == 0


def half_lanes(half):
    return pl.ds(pl.multiple_of(half * HALF_WIDE, HALF_WIDE), HALF_WIDE)


def half_pair(half, i):
    return pl.ds(pl.multiple_of(half * HALF_WIDE + i * LANES, LANES), LANES)


def two_rows(value, rows):
    wide = jnp.broadcast_to(value, (rows, LANES))
    high = wide.astype(BF16).astype(F32)
    return jnp.where(iota(0, (rows, LANES)) == 0, high, wide - high).astype(BF16)


def one_row(rows):
    rows = rows.astype(F32)
    return rows[0:1, :] + rows[1:2, :]


def load(pairs, sems):
    copies = [pltpu.make_async_copy(a, b, sems.at[i]) for i, (a, b) in enumerate(pairs)]
    for copy in copies:
        copy.start()
    return copies


def states_of_half(
    half, x_hbm, b_hbm, c_hbm, log_hbm, grad_hbm,
    x_ref, b_ref, c_ref, log_ref, grad_ref, end_ref, start_ref, sems,
):
    lanes = half_lanes(half)
    copies = load(
        [
            (log_hbm, log_ref),
            (b_hbm, b_ref),
            (c_hbm, c_ref),
            (x_hbm.at[:, lanes], x_ref),
            (grad_hbm.at[:, lanes], grad_ref),
        ],
        sems,
    )
    copies[0].wait()
    both = cumulative_columns(log_ref[...])
    lower_half = jnp.full((TOK, HEADS // 2), half, jnp.int32) == 0
    cum = jnp.where(lower_half, both[:, 0 : HEADS // 2], both[:, HEADS // 2 :])
    total = cum[TOK - 1 : TOK, :]
    to_end = jnp.exp(total - cum)
    from_start = jnp.exp(cum)
    last = jnp.exp(total)
    for i in range(PAIRS // 2):
        end_ref[:, pair(i)] = spread(to_end, i)
        start_ref[:, pair(i)] = spread(from_start, i)
    copies[1].wait()
    b_t = transposed(b_ref[...])
    copies[2].wait()
    c_t = transposed(c_ref[...])
    copies[3].wait()
    copies[4].wait()
    for i in range(PAIRS // 2):
        wx = (x_ref[:, pair(i)].astype(F32) * end_ref[:, pair(i)]).astype(BF16)
        wg = (grad_ref[:, pair(i)].astype(F32) * start_ref[:, pair(i)]).astype(BF16)
        yield i, nn(b_t, wx), nn(c_t, wg), spread(last, i)


def their_states_kernel(x_hbm, b_hbm, c_hbm, log_hbm, grad_hbm, send_ref, *scratch):
    for i, ends, opens, factor in states_of_half(
        1 - core(), x_hbm, b_hbm, c_hbm, log_hbm, grad_hbm, *scratch
    ):
        send_ref[0:TOK, pair(i)] = ends.astype(BF16)
        send_ref[TOK : 2 * TOK, pair(i)] = opens.astype(BF16)
        send_ref[2 * TOK : 2 * TOK + TAIL, pair(i)] = two_rows(factor, TAIL)


def my_states_kernel(x_hbm, b_hbm, c_hbm, log_hbm, grad_hbm, mine_ref, factor_ref, *scratch):
    for i, ends, opens, factor in states_of_half(
        core(), x_hbm, b_hbm, c_hbm, log_hbm, grad_hbm, *scratch
    ):
        mine_ref[0:TOK, pair(i)] = ends
        mine_ref[TOK : 2 * TOK, pair(i)] = opens
        factor_ref[:, pair(i)] = jnp.broadcast_to(factor, (8, LANES))


def chip_kernel(got_ref, mine_ref, factor_ref, send_hbm, send_ref, sems):
    first = first_core((TOK, LANES))
    first_row = first_core((1, LANES))
    copies = []
    for i in range(PAIRS // 2):
        mine = factor_ref[0:1, pair(i)]
        theirs = one_row(got_ref[2 * TOK : 2 * TOK + TAIL, pair(i)])
        factor0 = jnp.where(first_row, mine, theirs)
        factor1 = jnp.where(first_row, theirs, mine)
        my_ends = mine_ref[0:TOK, pair(i)]
        my_opens = mine_ref[TOK : 2 * TOK, pair(i)]
        ends = got_ref[0:TOK, pair(i)].astype(F32)
        opens = got_ref[TOK : 2 * TOK, pair(i)].astype(F32)
        chip_ends = factor1 * jnp.where(first, my_ends, ends) + jnp.where(first, ends, my_ends)
        chip_opens = factor0 * jnp.where(first, opens, my_opens) + jnp.where(first, my_opens, opens)
        chip_ends = chip_ends.astype(BF16)
        chip_opens = chip_opens.astype(BF16)
        factors = two_rows(mine * theirs, 8)
        for r in range(CHUNKS):
            rows = slice(r * ROWS, (r + 1) * ROWS)
            send_ref[i * CHUNKS + r] = jnp.concatenate(
                [chip_ends[rows], chip_opens[rows], factors], axis=0
            )
        owners = pl.ds(i * CHUNKS, CHUNKS)
        copies.append(pltpu.make_async_copy(send_ref.at[owners], send_hbm.at[owners], sems.at[i]))
        copies[i].start()
    for copy in copies:
        copy.wait()


def recurrence_kernel(got_ref, back_ref):
    count = got_ref.shape[0]
    entry = jnp.zeros((ROWS, LANES), F32)
    adjoint = jnp.zeros((ROWS, LANES), F32)
    entries, adjoints = [None] * count, [None] * count
    for k in range(count):
        m = count - 1 - k
        entries[k], adjoints[m] = entry, adjoint
        entry = one_row(got_ref[k, 2 * ROWS : SEND_ROWS]) * entry + got_ref[k, 0:ROWS].astype(F32)
        adjoint = one_row(got_ref[m, 2 * ROWS : SEND_ROWS]) * adjoint + got_ref[
            m, ROWS : 2 * ROWS
        ].astype(F32)
    for k in range(count):
        overlap = jnp.sum(entries[k] * adjoints[k], axis=0, keepdims=True)
        back_ref[k] = jnp.concatenate(
            [entries[k].astype(BF16), adjoints[k].astype(BF16), two_rows(overlap, 8)], axis=0
        )


def intra_kernel(
    x_hbm, b_hbm, c_hbm, log_hbm, grad_hbm,
    gx_ref, decay_ref, bc_ref, wx_ref, wg_ref, mats_ref, end_ref,
    x_ref, b_ref, c_ref, log_ref, grad_ref, sems,
):
    copies = load(
        [(log_hbm, log_ref), (b_hbm, b_ref), (c_hbm, c_ref), (x_hbm, x_ref), (grad_hbm, grad_ref)],
        sems,
    )
    for copy in copies:
        copy.wait()
    log_decay = log_ref[...]
    upper = (iota(0) <= iota(1)).astype(F32)
    cum_rows = nn(log_decay, upper, HIGHEST)
    cum = cumulative_columns(log_decay)
    to_end = jnp.exp(cum[TOK - 1 : TOK, :] - cum)
    from_start = jnp.exp(cum)
    b_mat = b_ref[...]
    c_mat = c_ref[...]
    mats_ref[0] = b_mat
    mats_ref[1] = c_mat
    scores = nt(b_mat, c_mat)
    later = iota(1) >= iota(0)
    before = iota(0) < iota(1)
    ends_after = (iota(0) >= iota(1)).astype(BF16)
    left = iota(1) < HALF
    mixed_sum = jnp.zeros((TOK, TOK), F32)
    for g in range(PAIRS):
        x_g = x_ref[:, pair(g)]
        grad_g = grad_ref[:, pair(g)]
        end_g = spread(to_end, g)
        end_ref[:, pair(g)] = end_g
        wx_ref[:, pair(g)] = (x_g.astype(F32) * end_g).astype(BF16)
        wg_ref[:, pair(g)] = (grad_g.astype(F32) * spread(from_start, g)).astype(BF16)
        grad_x = jnp.zeros((TOK, LANES), F32)
        for j in range(2):
            h = 2 * g + j
            mine = left if j == 0 else jnp.logical_not(left)
            x_h = jnp.where(mine, x_g, jnp.zeros_like(x_g))
            grad_h = jnp.where(mine, grad_g, jnp.zeros_like(grad_g))
            pairs = nt(x_h, grad_g)
            gaps = cum_rows[h : h + 1, :] - cum[:, h : h + 1]
            decays = jnp.exp(jnp.where(later, gaps, -1e4))
            kernel = decays * scores
            mixed_sum = mixed_sum + decays * pairs
            grad_x = grad_x + nn(kernel.astype(BF16), grad_h)
            reach = nn((kernel * pairs).astype(BF16), ends_after)
            decay_ref[h : h + 1, :] = jnp.sum(
                jnp.where(before, reach, 0.0), axis=0, keepdims=True
            )
        gx_ref[:, pair(g)] = grad_x
    high, low = split(mixed_sum)
    high_t, low_t = split(mixed_sum.T)
    bc_ref[0] = nn(high, c_mat) + nn(low, c_mat)
    bc_ref[1] = nn(high_t, b_mat) + nn(low_t, b_mat)


def slices(ref, i, start, rows):
    return ref[i * CHUNKS : (i + 1) * CHUNKS, start : start + rows, :]


def block_states(mine, back_ref, got_ref, mine_ref, factor_ref, out_ref):
    inside_is_adjoint = first_core((TOK, LANES)) == mine
    for i in range(PAIRS // 2):
        my_factor = factor_ref[0:1, pair(i)]
        their_factor = one_row(got_ref[2 * TOK : 2 * TOK + TAIL, pair(i)])
        entry = slices(back_ref, i, 0, ROWS).reshape(TOK, LANES).astype(F32)
        adjoint = slices(back_ref, i, ROWS, ROWS).reshape(TOK, LANES).astype(F32)
        chip = one_row(jnp.sum(slices(back_ref, i, 2 * ROWS, 8).astype(F32), axis=0))
        if mine:
            opens = got_ref[TOK : 2 * TOK, pair(i)].astype(F32)
            ends = got_ref[0:TOK, pair(i)].astype(F32)
        else:
            opens = mine_ref[TOK : 2 * TOK, pair(i)]
            ends = mine_ref[0:TOK, pair(i)]
        beyond, here, added = (
            jnp.where(inside_is_adjoint, a, b)
            for a, b in ((adjoint, entry), (entry, adjoint), (opens, ends))
        )
        factor, block_factor = (
            (their_factor, my_factor) if mine else (my_factor, their_factor)
        )
        inside = factor * beyond + added
        constant = block_factor * (factor * chip + jnp.sum(here * added, axis=0, keepdims=True))
        out_ref[0:TOK, pair(i)] = jnp.where(inside_is_adjoint, here, inside).astype(BF16)
        out_ref[TOK : 2 * TOK, pair(i)] = jnp.where(inside_is_adjoint, inside, here).astype(BF16)
        out_ref[2 * TOK : 2 * TOK + TAIL, pair(i)] = two_rows(constant, TAIL)


def half_sums(half, state_ref, wx_ref, wg_ref, b_sum, c_sum):
    for i in range(PAIRS // 2):
        lanes = half_pair(half, i)
        b_sum = b_sum + nt(wx_ref[:, lanes], state_ref[TOK : 2 * TOK, pair(i)])
        c_sum = c_sum + nt(wg_ref[:, lanes], state_ref[0:TOK, pair(i)])
    return b_sum, c_sum


def their_block_kernel(back_ref, got_ref, mine_ref, factor_ref, state_ref):
    block_states(False, back_ref, got_ref, mine_ref, factor_ref, state_ref)


def my_block_kernel(
    back_ref, got_ref, mine_ref, factor_ref, wx_ref, wg_ref, bc_ref, state_ref, part_ref
):
    block_states(True, back_ref, got_ref, mine_ref, factor_ref, state_ref)
    part_ref[0], part_ref[1] = half_sums(core(), state_ref, wx_ref, wg_ref, bc_ref[0], bc_ref[1])


def sums_kernel(other_ref, wx_ref, wg_ref, part_ref, send_hbm, sum_ref, sems):
    b_sum, c_sum = half_sums(1 - core(), other_ref, wx_ref, wg_ref, part_ref[0], part_ref[1])
    sum_ref[0:TOK, :] = b_sum.astype(BF16)
    sum_ref[TOK : 2 * TOK, :] = c_sum.astype(BF16)
    copies = load([(sum_ref, send_hbm.at[z]) for z in range(send_hbm.shape[0])], sems)
    for copy in copies:
        copy.wait()


def grads_kernel(
    own_ref, other_ref, wx_ref, wg_ref, mats_ref, gx_ref, inner_ref, end_ref, out_ref, decay_ref
):
    b_mat = mats_ref[0]
    c_mat = mats_ref[1]
    last = iota(0) == TOK - 1
    alphas = jnp.zeros((TOK, LANES), F32)
    betas = jnp.zeros((TOK, LANES), F32)
    for half, state_ref in ((core(), own_ref), (1 - core(), other_ref)):
        for i in range(PAIRS // 2):
            lanes = half_pair(half, i)
            from_adjoint = nn(b_mat, state_ref[TOK : 2 * TOK, pair(i)])
            out_ref[:, lanes] = (gx_ref[:, lanes] + end_ref[:, lanes] * from_adjoint).astype(BF16)
            beta = wx_ref[:, lanes].astype(F32) * from_adjoint
            alpha = wg_ref[:, lanes].astype(F32) * nn(c_mat, state_ref[0:TOK, pair(i)])
            constant = one_row(state_ref[2 * TOK : 2 * TOK + TAIL, pair(i)])
            alpha = alpha + jnp.where(last, constant, 0.0)
            head = 2 * (half * (PAIRS // 2) + i)
            pick = (iota(1) == head + iota(0) // HALF).astype(BF16)
            beta_high, beta_low = split(beta)
            alpha_high, alpha_low = split(alpha)
            betas = betas + nn(beta_high, pick) + nn(beta_low, pick)
            alphas = alphas + nn(alpha_high, pick) + nn(alpha_low, pick)
    after = (iota(0) <= iota(1)).astype(F32)
    before = (iota(0) > iota(1)).astype(F32)
    decay = nn(after, alphas, HIGHEST) + nn(before, betas, HIGHEST)
    decay_ref[...] = inner_ref[...] + decay.T[0:HEADS, :]


def head_sum_kernel(parts_ref, b_ref, c_ref):
    b_ref[...] = jnp.sum(parts_ref[:, 0:TOK, :].astype(F32), axis=0).astype(BF16)
    c_ref[...] = jnp.sum(parts_ref[:, TOK : 2 * TOK, :].astype(F32), axis=0).astype(BF16)


HBM_SPEC = pl.BlockSpec(memory_space=pltpu.HBM)


def call(body, outs, micros, *args, from_hbm=False, to_hbm=False, scratch=()):
    more = {}
    if from_hbm:
        more["in_specs"] = [HBM_SPEC] * len(args)
        args = [pltpu.with_memory_space_constraint(a, pltpu.HBM) for a in args]
    if to_hbm:
        more["out_specs"] = [HBM_SPEC] * len(outs)
    return pl.pallas_call(
        body,
        out_shape=[jax.ShapeDtypeStruct(s, d) for s, d in outs],
        scratch_shapes=list(scratch),
        compiler_params=pltpu.CompilerParams(vmem_limit_bytes=24 * 1024 * 1024),
        cost_estimate=pl.CostEstimate(
            flops=int(micros * 1e9), bytes_accessed=1 << 18, transcendentals=0
        ),
        **more,
    )(*args)


def per_device(seq, heads, x, b_mat, c_mat, log_decay, grad):
    chips = seq // 2
    assert chips == PAIRS // 2 * CHUNKS
    inputs = (x, b_mat, c_mat, log_decay, grad)
    swap = [(i, i ^ 1) for i in range(seq)]
    same_core = [[2 * m + c for m in range(chips)] for c in range(2)]
    wide = (TOK, WIDE)
    half = (TOK, HALF_WIDE)
    states = (2 * TOK + TAIL, HALF_WIDE)
    slices_shape = (chips, SEND_ROWS, LANES)

    def loaded(shape):
        return (
            pltpu.VMEM(shape, BF16),
            pltpu.VMEM((TOK, LANES), BF16),
            pltpu.VMEM((TOK, LANES), BF16),
            pltpu.VMEM((HEADS, TOK), F32),
            pltpu.VMEM(shape, BF16),
        )

    for_states = loaded(half) + (
        pltpu.VMEM(half, F32),
        pltpu.VMEM(half, F32),
        pltpu.SemaphoreType.DMA((5,)),
    )
    (send,) = call(
        their_states_kernel, [(states, BF16)], 1, *inputs, from_hbm=True, scratch=for_states
    )
    got = lax.ppermute(send, "seq", swap)
    mine, factor = call(
        my_states_kernel,
        [((2 * TOK, HALF_WIDE), F32), ((8, HALF_WIDE), F32)],
        1,
        *inputs,
        from_hbm=True,
        scratch=for_states,
    )
    (send,) = call(
        chip_kernel,
        [(slices_shape, BF16)],
        1,
        got,
        mine,
        factor,
        to_hbm=True,
        scratch=(pltpu.VMEM(slices_shape, BF16), pltpu.SemaphoreType.DMA((PAIRS // 2,))),
    )
    gathered = lax.all_to_all(send, "seq", 0, 0, tiled=True, axis_index_groups=same_core)
    local = call(
        intra_kernel,
        [
            (wide, F32),
            ((HEADS, TOK), F32),
            ((2, TOK, LANES), F32),
            (wide, BF16),
            (wide, BF16),
            ((2, TOK, LANES), BF16),
            (wide, F32),
        ],
        3,
        *inputs,
        from_hbm=True,
        scratch=loaded(wide) + (pltpu.SemaphoreType.DMA((5,)),),
    )
    gathered, (gx, inner, bc, wx, wg, mats, end) = lax.optimization_barrier((gathered, local))
    (back,) = call(recurrence_kernel, [(slices_shape, BF16)], 1, gathered)
    back = lax.all_to_all(back, "seq", 0, 0, tiled=True, axis_index_groups=same_core)
    (send,) = call(their_block_kernel, [(states, BF16)], 1, back, got, mine, factor)
    other = lax.ppermute(send, "seq", swap)
    own, part = call(
        my_block_kernel,
        [(states, BF16), ((2, TOK, LANES), F32)],
        1, back, got, mine, factor, wx, wg, bc,
    )
    (parts,) = call(
        sums_kernel,
        [((heads, 2 * TOK, LANES), BF16)],
        1,
        other,
        wx,
        wg,
        part,
        to_hbm=True,
        scratch=(pltpu.VMEM((2 * TOK, LANES), BF16), pltpu.SemaphoreType.DMA((heads,))),
    )
    parts = lax.all_to_all(parts, "head", 0, 0, tiled=True)
    grad_x, decay_grad = call(
        grads_kernel,
        [(wide, BF16), ((HEADS, TOK), F32)],
        3,
        own, other, wx, wg, mats, gx, inner, end,
    )
    parts, grad_x, decay_grad = lax.optimization_barrier((parts, grad_x, decay_grad))
    grad_b, grad_c = call(head_sum_kernel, [((TOK, LANES), BF16)] * 2, 1, parts)
    return grad_x, grad_b, grad_c, decay_grad


def solution(mesh):
    in_specs = (
        P("seq", "head"),
        P("seq", None),
        P("seq", None),
        P("head", "seq"),
        P("seq", "head"),
    )
    out_specs = (P("seq", "head"), P("seq", None), P("seq", None), P("head", "seq"))
    return jax.shard_map(
        functools.partial(per_device, mesh.shape["seq"], mesh.shape["head"]),
        mesh=mesh,
        in_specs=in_specs,
        out_specs=out_specs,
        check_vma=False,
    )
```

```python
import functools

import jax
import jax.numpy as jnp
from jax import lax
from jax.experimental import pallas as pl
from jax.experimental.pallas import tpu as pltpu
from jax.sharding import PartitionSpec as P

F32 = jnp.float32
BF16 = jnp.bfloat16
HIGHEST = lax.Precision.HIGHEST
TOK = 128
LANES = 128
HALF = 64
HEADS = 16
WIDE = HEADS * HALF
HALF_WIDE = WIDE // 2
PAIRS = 8
CHUNKS = 8
ROWS = 16
SEND_ROWS = 2 * ROWS + 8
TAIL = 16


def nn(a, b, precision=None):
    return lax.dot_general(
        a, b, (((1,), (0,)), ((), ())), precision=precision, preferred_element_type=F32
    )


def nt(a, b, precision=None):
    return lax.dot_general(
        a, b, (((1,), (1,)), ((), ())), precision=precision, preferred_element_type=F32
    )


def iota(dim, shape=(TOK, LANES)):
    return lax.broadcasted_iota(jnp.int32, shape, dim)


def pair(g):
    return slice(g * LANES, (g + 1) * LANES)


def transposed(matrix):
    return matrix.astype(F32).T.astype(BF16)


def split(value):
    high = value.astype(BF16)
    return high, (value - high.astype(F32)).astype(BF16)


def cumulative_columns(log_decay):
    lower = (iota(0) >= iota(1)).astype(F32)
    return nt(lower, log_decay, HIGHEST)


def spread(columns, g):
    rows = columns.shape[0]
    left = iota(1, (rows, LANES)) < HALF
    a = jnp.broadcast_to(columns[:, 2 * g : 2 * g + 1], (rows, LANES))
    b = jnp.broadcast_to(columns[:, 2 * g + 1 : 2 * g + 2], (rows, LANES))
    return jnp.where(left, a, b)


def core():
    return lax.axis_index("seq") % 2


def first_core(shape):
    return jnp.full(shape, core(), jnp.int32) == 0


def half_lanes(half):
    return pl.ds(pl.multiple_of(half * HALF_WIDE, HALF_WIDE), HALF_WIDE)


def half_pair(half, i):
    return pl.ds(pl.multiple_of(half * HALF_WIDE + i * LANES, LANES), LANES)


def two_rows(value, rows):
    wide = jnp.broadcast_to(value, (rows, LANES))
    high = wide.astype(BF16).astype(F32)
    return jnp.where(iota(0, (rows, LANES)) == 0, high, wide - high).astype(BF16)


def one_row(rows):
    rows = rows.astype(F32)
    return rows[0:1, :] + rows[1:2, :]


def load(pairs, sems):
    copies = [pltpu.make_async_copy(a, b, sems.at[i]) for i, (a, b) in enumerate(pairs)]
    for copy in copies:
        copy.start()
    return copies


def states_of_half(cum, b_t, c_t, x_ref, grad_ref, end_ref, start_ref, copies=()):
    total = cum[TOK - 1 : TOK, :]
    to_end = jnp.exp(total - cum)
    from_start = jnp.exp(cum)
    last = jnp.exp(total)
    for i in range(PAIRS // 2):
        end_ref[:, pair(i)] = spread(to_end, i)
        start_ref[:, pair(i)] = spread(from_start, i)
    for copy in copies:
        copy.wait()
    for i in range(PAIRS // 2):
        wx = (x_ref[:, pair(i)].astype(F32) * end_ref[:, pair(i)]).astype(BF16)
        wg = (grad_ref[:, pair(i)].astype(F32) * start_ref[:, pair(i)]).astype(BF16)
        yield i, nn(b_t, wx), nn(c_t, wg), spread(last, i)


def their_states_kernel(
    x_hbm, b_hbm, c_hbm, log_hbm, grad_hbm,
    send_ref, x_mine, grad_mine, cum_mine, b_t_ref, c_t_ref,
    x_ref, b_ref, c_ref, log_ref, grad_ref, end_ref, start_ref, sems,
):
    theirs = half_lanes(1 - core())
    mine = half_lanes(core())
    copies = load(
        [
            (log_hbm, log_ref),
            (b_hbm, b_ref),
            (c_hbm, c_ref),
            (x_hbm.at[:, theirs], x_ref),
            (grad_hbm.at[:, theirs], grad_ref),
            (x_hbm.at[:, mine], x_mine),
            (grad_hbm.at[:, mine], grad_mine),
        ],
        sems,
    )
    copies[0].wait()
    both = cumulative_columns(log_ref[...])
    lower, upper = both[:, 0 : HEADS // 2], both[:, HEADS // 2 :]
    lower_mine = first_core((TOK, HEADS // 2))
    cum_mine[...] = jnp.where(lower_mine, lower, upper)
    copies[1].wait()
    b_t = transposed(b_ref[...])
    b_t_ref[...] = b_t
    copies[2].wait()
    c_t = transposed(c_ref[...])
    c_t_ref[...] = c_t
    for i, ends, opens, factor in states_of_half(
        jnp.where(lower_mine, upper, lower),
        b_t, c_t, x_ref, grad_ref, end_ref, start_ref, copies[3:5],
    ):
        send_ref[0:TOK, pair(i)] = ends.astype(BF16)
        send_ref[TOK : 2 * TOK, pair(i)] = opens.astype(BF16)
        send_ref[2 * TOK : 2 * TOK + TAIL, pair(i)] = two_rows(factor, TAIL)
    copies[5].wait()
    copies[6].wait()


def my_states_kernel(
    x_ref, grad_ref, cum_ref, b_t_ref, c_t_ref, mine_ref, factor_ref, end_ref, start_ref
):
    for i, ends, opens, factor in states_of_half(
        cum_ref[...], b_t_ref[...], c_t_ref[...], x_ref, grad_ref, end_ref, start_ref
    ):
        mine_ref[0:TOK, pair(i)] = ends
        mine_ref[TOK : 2 * TOK, pair(i)] = opens
        factor_ref[:, pair(i)] = jnp.broadcast_to(factor, (8, LANES))


def chip_kernel(got_ref, mine_ref, factor_ref, send_hbm, send_ref, sems):
    first = first_core((TOK, LANES))
    first_row = first_core((1, LANES))
    copies = []
    for i in range(PAIRS // 2):
        mine = factor_ref[0:1, pair(i)]
        theirs = one_row(got_ref[2 * TOK : 2 * TOK + TAIL, pair(i)])
        factor0 = jnp.where(first_row, mine, theirs)
        factor1 = jnp.where(first_row, theirs, mine)
        my_ends = mine_ref[0:TOK, pair(i)]
        my_opens = mine_ref[TOK : 2 * TOK, pair(i)]
        ends = got_ref[0:TOK, pair(i)].astype(F32)
        opens = got_ref[TOK : 2 * TOK, pair(i)].astype(F32)
        chip_ends = factor1 * jnp.where(first, my_ends, ends) + jnp.where(first, ends, my_ends)
        chip_opens = factor0 * jnp.where(first, opens, my_opens) + jnp.where(first, my_opens, opens)
        chip_ends = chip_ends.astype(BF16)
        chip_opens = chip_opens.astype(BF16)
        factors = two_rows(mine * theirs, 8)
        for r in range(CHUNKS):
            rows = slice(r * ROWS, (r + 1) * ROWS)
            send_ref[i * CHUNKS + r] = jnp.concatenate(
                [chip_ends[rows], chip_opens[rows], factors], axis=0
            )
        owners = pl.ds(i * CHUNKS, CHUNKS)
        copies.append(pltpu.make_async_copy(send_ref.at[owners], send_hbm.at[owners], sems.at[i]))
        copies[i].start()
    for copy in copies:
        copy.wait()


def recurrence_kernel(got_ref, back_ref):
    count = got_ref.shape[0]
    entry = jnp.zeros((ROWS, LANES), F32)
    adjoint = jnp.zeros((ROWS, LANES), F32)
    entries, adjoints = [None] * count, [None] * count
    for k in range(count):
        m = count - 1 - k
        entries[k], adjoints[m] = entry, adjoint
        entry = one_row(got_ref[k, 2 * ROWS : SEND_ROWS]) * entry + got_ref[k, 0:ROWS].astype(F32)
        adjoint = one_row(got_ref[m, 2 * ROWS : SEND_ROWS]) * adjoint + got_ref[
            m, ROWS : 2 * ROWS
        ].astype(F32)
    for k in range(count):
        overlap = jnp.sum(entries[k] * adjoints[k], axis=0, keepdims=True)
        back_ref[k] = jnp.concatenate(
            [entries[k].astype(BF16), adjoints[k].astype(BF16), two_rows(overlap, 8)], axis=0
        )


def intra_kernel(
    x_hbm, b_hbm, c_hbm, log_hbm, grad_hbm,
    gx_ref, decay_ref, bc_ref, wx_ref, wg_ref, mats_ref, end_ref,
    x_ref, b_ref, c_ref, log_ref, grad_ref, sems,
):
    copies = load(
        [(log_hbm, log_ref), (b_hbm, b_ref), (c_hbm, c_ref), (x_hbm, x_ref), (grad_hbm, grad_ref)],
        sems,
    )
    for copy in copies:
        copy.wait()
    log_decay = log_ref[...]
    upper = (iota(0) <= iota(1)).astype(F32)
    cum_rows = nn(log_decay, upper, HIGHEST)
    cum = cumulative_columns(log_decay)
    to_end = jnp.exp(cum[TOK - 1 : TOK, :] - cum)
    from_start = jnp.exp(cum)
    b_mat = b_ref[...]
    c_mat = c_ref[...]
    mats_ref[0] = b_mat
    mats_ref[1] = c_mat
    scores = nt(b_mat, c_mat)
    later = iota(1) >= iota(0)
    before = iota(0) < iota(1)
    ends_after = (iota(0) >= iota(1)).astype(BF16)
    left = iota(1) < HALF
    mixed_sum = jnp.zeros((TOK, TOK), F32)
    for g in range(PAIRS):
        x_g = x_ref[:, pair(g)]
        grad_g = grad_ref[:, pair(g)]
        end_g = spread(to_end, g)
        end_ref[:, pair(g)] = end_g
        wx_ref[:, pair(g)] = (x_g.astype(F32) * end_g).astype(BF16)
        wg_ref[:, pair(g)] = (grad_g.astype(F32) * spread(from_start, g)).astype(BF16)
        grad_x = jnp.zeros((TOK, LANES), F32)
        for j in range(2):
            h = 2 * g + j
            mine = left if j == 0 else jnp.logical_not(left)
            x_h = jnp.where(mine, x_g, jnp.zeros_like(x_g))
            grad_h = jnp.where(mine, grad_g, jnp.zeros_like(grad_g))
            pairs = nt(x_h, grad_g)
            gaps = cum_rows[h : h + 1, :] - cum[:, h : h + 1]
            decays = jnp.exp(jnp.where(later, gaps, -1e4))
            kernel = decays * scores
            mixed_sum = mixed_sum + decays * pairs
            grad_x = grad_x + nn(kernel.astype(BF16), grad_h)
            reach = nn((kernel * pairs).astype(BF16), ends_after)
            decay_ref[h : h + 1, :] = jnp.sum(
                jnp.where(before, reach, 0.0), axis=0, keepdims=True
            )
        gx_ref[:, pair(g)] = grad_x
    high, low = split(mixed_sum)
    high_t, low_t = split(mixed_sum.T)
    bc_ref[0] = nn(high, c_mat) + nn(low, c_mat)
    bc_ref[1] = nn(high_t, b_mat) + nn(low_t, b_mat)


def slices(ref, i, start, rows):
    return ref[i * CHUNKS : (i + 1) * CHUNKS, start : start + rows, :]


def block_states(mine, back_ref, got_ref, mine_ref, factor_ref, out_ref):
    inside_is_adjoint = first_core((TOK, LANES)) == mine
    for i in range(PAIRS // 2):
        my_factor = factor_ref[0:1, pair(i)]
        their_factor = one_row(got_ref[2 * TOK : 2 * TOK + TAIL, pair(i)])
        entry = slices(back_ref, i, 0, ROWS).reshape(TOK, LANES).astype(F32)
        adjoint = slices(back_ref, i, ROWS, ROWS).reshape(TOK, LANES).astype(F32)
        chip = one_row(jnp.sum(slices(back_ref, i, 2 * ROWS, 8).astype(F32), axis=0))
        if mine:
            opens = got_ref[TOK : 2 * TOK, pair(i)].astype(F32)
            ends = got_ref[0:TOK, pair(i)].astype(F32)
        else:
            opens = mine_ref[TOK : 2 * TOK, pair(i)]
            ends = mine_ref[0:TOK, pair(i)]
        beyond, here, added = (
            jnp.where(inside_is_adjoint, a, b)
            for a, b in ((adjoint, entry), (entry, adjoint), (opens, ends))
        )
        factor, block_factor = (
            (their_factor, my_factor) if mine else (my_factor, their_factor)
        )
        inside = factor * beyond + added
        constant = block_factor * (factor * chip + jnp.sum(here * added, axis=0, keepdims=True))
        out_ref[0:TOK, pair(i)] = jnp.where(inside_is_adjoint, here, inside).astype(BF16)
        out_ref[TOK : 2 * TOK, pair(i)] = jnp.where(inside_is_adjoint, inside, here).astype(BF16)
        out_ref[2 * TOK : 2 * TOK + TAIL, pair(i)] = two_rows(constant, TAIL)


def half_sum(half, state_ref, weighted_ref, start, total):
    for i in range(PAIRS // 2):
        total = total + nt(weighted_ref[:, half_pair(half, i)], state_ref[start : start + TOK, pair(i)])
    return total


def their_block_kernel(back_ref, got_ref, mine_ref, factor_ref, state_ref):
    block_states(False, back_ref, got_ref, mine_ref, factor_ref, state_ref)


def my_block_kernel(
    back_ref, got_ref, mine_ref, factor_ref, wx_ref, wg_ref, bc_ref, state_ref, part_ref
):
    block_states(True, back_ref, got_ref, mine_ref, factor_ref, state_ref)
    part_ref[0] = half_sum(core(), state_ref, wx_ref, TOK, bc_ref[0])
    part_ref[1] = half_sum(core(), state_ref, wg_ref, 0, bc_ref[1])


def sums_kernel(other_ref, wx_ref, wg_ref, part_ref, send_hbm, sum_ref, sems):
    count = send_hbm.shape[0]
    copies = []
    for k, (weighted_ref, start) in enumerate(((wx_ref, TOK), (wg_ref, 0))):
        total = half_sum(1 - core(), other_ref, weighted_ref, start, part_ref[k])
        rows = pl.ds(k * TOK, TOK)
        sum_ref[rows, :] = total.astype(BF16)
        copies += load(
            [(sum_ref.at[rows], send_hbm.at[z, rows]) for z in range(count)], sems.at[k]
        )
    for copy in copies:
        copy.wait()


def grads_kernel(
    own_ref, other_ref, wx_ref, wg_ref, mats_ref, gx_ref, inner_ref, end_ref, out_ref, decay_ref
):
    b_mat = mats_ref[0]
    c_mat = mats_ref[1]
    last = iota(0) == TOK - 1
    alphas = jnp.zeros((TOK, LANES), F32)
    betas = jnp.zeros((TOK, LANES), F32)
    for half, state_ref in ((core(), own_ref), (1 - core(), other_ref)):
        for i in range(PAIRS // 2):
            lanes = half_pair(half, i)
            from_adjoint = nn(b_mat, state_ref[TOK : 2 * TOK, pair(i)])
            out_ref[:, lanes] = (gx_ref[:, lanes] + end_ref[:, lanes] * from_adjoint).astype(BF16)
            beta = wx_ref[:, lanes].astype(F32) * from_adjoint
            alpha = wg_ref[:, lanes].astype(F32) * nn(c_mat, state_ref[0:TOK, pair(i)])
            constant = one_row(state_ref[2 * TOK : 2 * TOK + TAIL, pair(i)])
            alpha = alpha + jnp.where(last, constant, 0.0)
            head = 2 * (half * (PAIRS // 2) + i)
            pick = (iota(1) == head + iota(0) // HALF).astype(BF16)
            beta_high, beta_low = split(beta)
            alpha_high, alpha_low = split(alpha)
            betas = betas + nn(beta_high, pick) + nn(beta_low, pick)
            alphas = alphas + nn(alpha_high, pick) + nn(alpha_low, pick)
    after = (iota(0) <= iota(1)).astype(F32)
    before = (iota(0) > iota(1)).astype(F32)
    decay = nn(after, alphas, HIGHEST) + nn(before, betas, HIGHEST)
    decay_ref[...] = inner_ref[...] + decay.T[0:HEADS, :]


def head_sum_kernel(parts_ref, b_ref, c_ref):
    b_ref[...] = jnp.sum(parts_ref[:, 0:TOK, :].astype(F32), axis=0).astype(BF16)
    c_ref[...] = jnp.sum(parts_ref[:, TOK : 2 * TOK, :].astype(F32), axis=0).astype(BF16)


HBM_SPEC = pl.BlockSpec(memory_space=pltpu.HBM)


def call(body, outs, micros, *args, from_hbm=False, to_hbm=False, scratch=()):
    more = {}
    if from_hbm:
        more["in_specs"] = [HBM_SPEC] * len(args)
        args = [pltpu.with_memory_space_constraint(a, pltpu.HBM) for a in args]
    if to_hbm:
        more["out_specs"] = [HBM_SPEC] * len(outs)
    return pl.pallas_call(
        body,
        out_shape=[jax.ShapeDtypeStruct(s, d) for s, d in outs],
        scratch_shapes=list(scratch),
        compiler_params=pltpu.CompilerParams(vmem_limit_bytes=24 * 1024 * 1024),
        cost_estimate=pl.CostEstimate(
            flops=int(micros * 1e9), bytes_accessed=1 << 18, transcendentals=0
        ),
        **more,
    )(*args)


def per_device(seq, heads, x, b_mat, c_mat, log_decay, grad):
    chips = seq // 2
    assert chips == PAIRS // 2 * CHUNKS
    inputs = (x, b_mat, c_mat, log_decay, grad)
    swap = [(i, i ^ 1) for i in range(seq)]
    same_core = [[2 * m + c for m in range(chips)] for c in range(2)]
    wide = (TOK, WIDE)
    half = (TOK, HALF_WIDE)
    states = (2 * TOK + TAIL, HALF_WIDE)
    slices_shape = (chips, SEND_ROWS, LANES)

    def loaded(shape):
        return (
            pltpu.VMEM(shape, BF16),
            pltpu.VMEM((TOK, LANES), BF16),
            pltpu.VMEM((TOK, LANES), BF16),
            pltpu.VMEM((HEADS, TOK), F32),
            pltpu.VMEM(shape, BF16),
        )

    spreads = (pltpu.VMEM(half, F32), pltpu.VMEM(half, F32))
    square = ((TOK, LANES), BF16)
    send, *for_mine = call(
        their_states_kernel,
        [(states, BF16), (half, BF16), (half, BF16), ((TOK, HEADS // 2), F32), square, square],
        1,
        *inputs,
        from_hbm=True,
        scratch=loaded(half) + spreads + (pltpu.SemaphoreType.DMA((7,)),),
    )
    got = lax.ppermute(send, "seq", swap)
    mine, factor = call(
        my_states_kernel,
        [((2 * TOK, HALF_WIDE), F32), ((8, HALF_WIDE), F32)],
        1,
        *for_mine,
        scratch=spreads,
    )
    (send,) = call(
        chip_kernel,
        [(slices_shape, BF16)],
        1,
        got,
        mine,
        factor,
        to_hbm=True,
        scratch=(pltpu.VMEM(slices_shape, BF16), pltpu.SemaphoreType.DMA((PAIRS // 2,))),
    )
    gathered = lax.all_to_all(send, "seq", 0, 0, tiled=True, axis_index_groups=same_core)
    local = call(
        intra_kernel,
        [
            (wide, F32),
            ((HEADS, TOK), F32),
            ((2, TOK, LANES), F32),
            (wide, BF16),
            (wide, BF16),
            ((2, TOK, LANES), BF16),
            (wide, F32),
        ],
        3,
        *inputs,
        from_hbm=True,
        scratch=loaded(wide) + (pltpu.SemaphoreType.DMA((5,)),),
    )
    gathered, (gx, inner, bc, wx, wg, mats, end) = lax.optimization_barrier((gathered, local))
    (back,) = call(recurrence_kernel, [(slices_shape, BF16)], 1, gathered)
    back = lax.all_to_all(back, "seq", 0, 0, tiled=True, axis_index_groups=same_core)
    (send,) = call(their_block_kernel, [(states, BF16)], 1, back, got, mine, factor)
    other = lax.ppermute(send, "seq", swap)
    own, part = call(
        my_block_kernel,
        [(states, BF16), ((2, TOK, LANES), F32)],
        1, back, got, mine, factor, wx, wg, bc,
    )
    (parts,) = call(
        sums_kernel,
        [((heads, 2 * TOK, LANES), BF16)],
        1,
        other,
        wx,
        wg,
        part,
        to_hbm=True,
        scratch=(pltpu.VMEM((2 * TOK, LANES), BF16), pltpu.SemaphoreType.DMA((2, heads))),
    )
    parts = lax.all_to_all(parts, "head", 0, 0, tiled=True)
    grad_x, decay_grad = call(
        grads_kernel,
        [(wide, BF16), ((HEADS, TOK), F32)],
        3,
        own, other, wx, wg, mats, gx, inner, end,
    )
    parts, grad_x, decay_grad = lax.optimization_barrier((parts, grad_x, decay_grad))
    grad_b, grad_c = call(head_sum_kernel, [((TOK, LANES), BF16)] * 2, 1, parts)
    return grad_x, grad_b, grad_c, decay_grad


def solution(mesh):
    in_specs = (
        P("seq", "head"),
        P("seq", None),
        P("seq", None),
        P("head", "seq"),
        P("seq", "head"),
    )
    out_specs = (P("seq", "head"), P("seq", None), P("seq", None), P("head", "seq"))
    return jax.shard_map(
        functools.partial(per_device, mesh.shape["seq"], mesh.shape["head"]),
        mesh=mesh,
        in_specs=in_specs,
        out_specs=out_specs,
        check_vma=False,
    )
```

```python
import functools

import jax
import jax.numpy as jnp
from jax import lax
from jax.experimental import pallas as pl
from jax.experimental.pallas import tpu as pltpu
from jax.sharding import PartitionSpec as P

F32 = jnp.float32
BF16 = jnp.bfloat16
HIGHEST = lax.Precision.HIGHEST
TOK = 128
LANES = 128
HALF = 64
HEADS = 16
WIDE = HEADS * HALF
HALF_WIDE = WIDE // 2
PAIRS = 8
CHUNKS = 8
ROWS = 16
SEND_ROWS = 2 * ROWS + 2
SEND_TILES = SEND_ROWS // 2
TAIL = 16


def nn(a, b, precision=None):
    return lax.dot_general(
        a, b, (((1,), (0,)), ((), ())), precision=precision, preferred_element_type=F32
    )


def nt(a, b, precision=None):
    return lax.dot_general(
        a, b, (((1,), (1,)), ((), ())), precision=precision, preferred_element_type=F32
    )


def iota(dim, shape=(TOK, LANES)):
    return lax.broadcasted_iota(jnp.int32, shape, dim)


def pair(g):
    return slice(g * LANES, (g + 1) * LANES)


def transposed(matrix):
    return matrix.astype(F32).T.astype(BF16)


def split(value):
    high = value.astype(BF16)
    return high, (value - high.astype(F32)).astype(BF16)


def cumulative_columns(log_decay):
    lower = (iota(0) >= iota(1)).astype(F32)
    return nt(lower, log_decay, HIGHEST)


def spread(columns, g):
    rows = columns.shape[0]
    left = iota(1, (rows, LANES)) < HALF
    a = jnp.broadcast_to(columns[:, 2 * g : 2 * g + 1], (rows, LANES))
    b = jnp.broadcast_to(columns[:, 2 * g + 1 : 2 * g + 2], (rows, LANES))
    return jnp.where(left, a, b)


def core():
    return lax.axis_index("seq") % 2


def first_core(shape):
    return jnp.full(shape, core(), jnp.int32) == 0


def half_lanes(half):
    return pl.ds(pl.multiple_of(half * HALF_WIDE, HALF_WIDE), HALF_WIDE)


def half_pair(half, i):
    return pl.ds(pl.multiple_of(half * HALF_WIDE + i * LANES, LANES), LANES)


def two_rows(value, rows):
    wide = jnp.broadcast_to(value, (rows, LANES))
    high = wide.astype(BF16).astype(F32)
    return jnp.where(iota(0, (rows, LANES)) == 0, high, wide - high).astype(BF16)


def one_row(rows):
    rows = rows.astype(F32)
    return rows[0:1, :] + rows[1:2, :]


def put(ref, k, rows):
    for j in range(SEND_TILES):
        ref[k, j] = rows[2 * j : 2 * j + 2]


def take(ref, k):
    return ref[k].reshape(SEND_ROWS, LANES)


def load(pairs, sems):
    copies = [pltpu.make_async_copy(a, b, sems.at[i]) for i, (a, b) in enumerate(pairs)]
    for copy in copies:
        copy.start()
    return copies


def states_of_half(cum, b_t, c_t, x_ref, grad_ref, end_ref, start_ref, copies=()):
    total = cum[TOK - 1 : TOK, :]
    to_end = jnp.exp(total - cum)
    from_start = jnp.exp(cum)
    last = jnp.exp(total)
    for i in range(PAIRS // 2):
        end_ref[:, pair(i)] = spread(to_end, i)
        start_ref[:, pair(i)] = spread(from_start, i)
    for copy in copies:
        copy.wait()
    for i in range(PAIRS // 2):
        wx = (x_ref[:, pair(i)].astype(F32) * end_ref[:, pair(i)]).astype(BF16)
        wg = (grad_ref[:, pair(i)].astype(F32) * start_ref[:, pair(i)]).astype(BF16)
        yield i, nn(b_t, wx), nn(c_t, wg), spread(last, i)


def their_states_kernel(
    x_hbm, b_hbm, c_hbm, log_hbm, grad_hbm,
    send_ref, x_mine, grad_mine, cum_mine, b_t_ref, c_t_ref,
    x_ref, b_ref, c_ref, log_ref, grad_ref, end_ref, start_ref, sems,
):
    theirs = half_lanes(1 - core())
    mine = half_lanes(core())
    copies = load(
        [
            (log_hbm, log_ref),
            (b_hbm, b_ref),
            (c_hbm, c_ref),
            (x_hbm.at[:, theirs], x_ref),
            (grad_hbm.at[:, theirs], grad_ref),
            (x_hbm.at[:, mine], x_mine),
            (grad_hbm.at[:, mine], grad_mine),
        ],
        sems,
    )
    copies[0].wait()
    both = cumulative_columns(log_ref[...])
    lower, upper = both[:, 0 : HEADS // 2], both[:, HEADS // 2 :]
    lower_mine = first_core((TOK, HEADS // 2))
    cum_mine[...] = jnp.where(lower_mine, lower, upper)
    copies[1].wait()
    b_t = transposed(b_ref[...])
    b_t_ref[...] = b_t
    copies[2].wait()
    c_t = transposed(c_ref[...])
    c_t_ref[...] = c_t
    for i, ends, opens, factor in states_of_half(
        jnp.where(lower_mine, upper, lower),
        b_t, c_t, x_ref, grad_ref, end_ref, start_ref, copies[3:5],
    ):
        send_ref[0:TOK, pair(i)] = ends.astype(BF16)
        send_ref[TOK : 2 * TOK, pair(i)] = opens.astype(BF16)
        send_ref[2 * TOK : 2 * TOK + TAIL, pair(i)] = two_rows(factor, TAIL)
    copies[5].wait()
    copies[6].wait()


def my_states_kernel(
    x_ref, grad_ref, cum_ref, b_t_ref, c_t_ref, mine_ref, factor_ref, end_ref, start_ref
):
    for i, ends, opens, factor in states_of_half(
        cum_ref[...], b_t_ref[...], c_t_ref[...], x_ref, grad_ref, end_ref, start_ref
    ):
        mine_ref[0:TOK, pair(i)] = ends
        mine_ref[TOK : 2 * TOK, pair(i)] = opens
        factor_ref[:, pair(i)] = jnp.broadcast_to(factor, (8, LANES))


def chip_kernel(got_ref, mine_ref, factor_ref, send_hbm, send_ref, sems):
    first = first_core((TOK, LANES))
    first_row = first_core((1, LANES))
    copies = []
    for i in range(PAIRS // 2):
        mine = factor_ref[0:1, pair(i)]
        theirs = one_row(got_ref[2 * TOK : 2 * TOK + TAIL, pair(i)])
        factor0 = jnp.where(first_row, mine, theirs)
        factor1 = jnp.where(first_row, theirs, mine)
        my_ends = mine_ref[0:TOK, pair(i)]
        my_opens = mine_ref[TOK : 2 * TOK, pair(i)]
        ends = got_ref[0:TOK, pair(i)].astype(F32)
        opens = got_ref[TOK : 2 * TOK, pair(i)].astype(F32)
        chip_ends = factor1 * jnp.where(first, my_ends, ends) + jnp.where(first, ends, my_ends)
        chip_opens = factor0 * jnp.where(first, opens, my_opens) + jnp.where(first, my_opens, opens)
        chip_ends = chip_ends.astype(BF16)
        chip_opens = chip_opens.astype(BF16)
        factors = two_rows(mine * theirs, 2)
        for r in range(CHUNKS):
            rows = slice(r * ROWS, (r + 1) * ROWS)
            block = jnp.concatenate([chip_ends[rows], chip_opens[rows], factors], axis=0)
            put(send_ref, i * CHUNKS + r, block)
        owners = pl.ds(i * CHUNKS, CHUNKS)
        copies.append(pltpu.make_async_copy(send_ref.at[owners], send_hbm.at[owners], sems.at[i]))
        copies[i].start()
    for copy in copies:
        copy.wait()


def recurrence_kernel(got_ref, back_ref):
    count = got_ref.shape[0]
    entry = jnp.zeros((ROWS, LANES), F32)
    adjoint = jnp.zeros((ROWS, LANES), F32)
    blocks = [take(got_ref, k) for k in range(count)]
    entries, adjoints = [None] * count, [None] * count
    for k in range(count):
        m = count - 1 - k
        entries[k], adjoints[m] = entry, adjoint
        entry = one_row(blocks[k][2 * ROWS :]) * entry + blocks[k][0:ROWS].astype(F32)
        adjoint = one_row(blocks[m][2 * ROWS :]) * adjoint + blocks[m][ROWS : 2 * ROWS].astype(F32)
    for k in range(count):
        overlap = jnp.sum(entries[k] * adjoints[k], axis=0, keepdims=True)
        block = [entries[k].astype(BF16), adjoints[k].astype(BF16), two_rows(overlap, 2)]
        put(back_ref, k, jnp.concatenate(block, axis=0))


def intra_kernel(
    x_hbm, b_hbm, c_hbm, log_hbm, grad_hbm,
    gx_ref, decay_ref, bc_ref, wx_ref, wg_ref, mats_ref, end_ref,
    x_ref, b_ref, c_ref, log_ref, grad_ref, sems,
):
    copies = load(
        [(log_hbm, log_ref), (b_hbm, b_ref), (c_hbm, c_ref), (x_hbm, x_ref), (grad_hbm, grad_ref)],
        sems,
    )
    for copy in copies:
        copy.wait()
    log_decay = log_ref[...]
    upper = (iota(0) <= iota(1)).astype(F32)
    cum_rows = nn(log_decay, upper, HIGHEST)
    cum = cumulative_columns(log_decay)
    to_end = jnp.exp(cum[TOK - 1 : TOK, :] - cum)
    from_start = jnp.exp(cum)
    b_mat = b_ref[...]
    c_mat = c_ref[...]
    mats_ref[0] = b_mat
    mats_ref[1] = c_mat
    scores = nt(b_mat, c_mat)
    later = iota(1) >= iota(0)
    before = iota(0) < iota(1)
    ends_after = (iota(0) >= iota(1)).astype(BF16)
    left = iota(1) < HALF
    mixed_sum = jnp.zeros((TOK, TOK), F32)
    for g in range(PAIRS):
        x_g = x_ref[:, pair(g)]
        grad_g = grad_ref[:, pair(g)]
        end_g = spread(to_end, g)
        end_ref[:, pair(g)] = end_g
        wx_ref[:, pair(g)] = (x_g.astype(F32) * end_g).astype(BF16)
        wg_ref[:, pair(g)] = (grad_g.astype(F32) * spread(from_start, g)).astype(BF16)
        grad_x = jnp.zeros((TOK, LANES), F32)
        for j in range(2):
            h = 2 * g + j
            mine = left if j == 0 else jnp.logical_not(left)
            x_h = jnp.where(mine, x_g, jnp.zeros_like(x_g))
            grad_h = jnp.where(mine, grad_g, jnp.zeros_like(grad_g))
            pairs = nt(x_h, grad_g)
            gaps = cum_rows[h : h + 1, :] - cum[:, h : h + 1]
            decays = jnp.exp(jnp.where(later, gaps, -1e4))
            kernel = decays * scores
            mixed_sum = mixed_sum + decays * pairs
            grad_x = grad_x + nn(kernel.astype(BF16), grad_h)
            reach = nn((kernel * pairs).astype(BF16), ends_after)
            decay_ref[h : h + 1, :] = jnp.sum(
                jnp.where(before, reach, 0.0), axis=0, keepdims=True
            )
        gx_ref[:, pair(g)] = grad_x
    high, low = split(mixed_sum)
    high_t, low_t = split(mixed_sum.T)
    bc_ref[0] = nn(high, c_mat) + nn(low, c_mat)
    bc_ref[1] = nn(high_t, b_mat) + nn(low_t, b_mat)


def block_states(mine, back_ref, got_ref, mine_ref, factor_ref, out_ref):
    inside_is_adjoint = first_core((TOK, LANES)) == mine
    for i in range(PAIRS // 2):
        my_factor = factor_ref[0:1, pair(i)]
        their_factor = one_row(got_ref[2 * TOK : 2 * TOK + TAIL, pair(i)])
        blocks = [take(back_ref, i * CHUNKS + r) for r in range(CHUNKS)]
        entry = jnp.concatenate([block[0:ROWS] for block in blocks], axis=0).astype(F32)
        adjoint = jnp.concatenate([block[ROWS : 2 * ROWS] for block in blocks], axis=0).astype(F32)
        chip = sum(one_row(block[2 * ROWS :]) for block in blocks)
        if mine:
            opens = got_ref[TOK : 2 * TOK, pair(i)].astype(F32)
            ends = got_ref[0:TOK, pair(i)].astype(F32)
        else:
            opens = mine_ref[TOK : 2 * TOK, pair(i)]
            ends = mine_ref[0:TOK, pair(i)]
        beyond, here, added = (
            jnp.where(inside_is_adjoint, a, b)
            for a, b in ((adjoint, entry), (entry, adjoint), (opens, ends))
        )
        factor, block_factor = (
            (their_factor, my_factor) if mine else (my_factor, their_factor)
        )
        inside = factor * beyond + added
        constant = block_factor * (factor * chip + jnp.sum(here * added, axis=0, keepdims=True))
        out_ref[0:TOK, pair(i)] = jnp.where(inside_is_adjoint, here, inside).astype(BF16)
        out_ref[TOK : 2 * TOK, pair(i)] = jnp.where(inside_is_adjoint, inside, here).astype(BF16)
        out_ref[2 * TOK : 2 * TOK + TAIL, pair(i)] = two_rows(constant, TAIL)


def half_sum(half, state_ref, weighted_ref, start, total):
    for i in range(PAIRS // 2):
        total = total + nt(weighted_ref[:, half_pair(half, i)], state_ref[start : start + TOK, pair(i)])
    return total


def their_block_kernel(back_ref, got_ref, mine_ref, factor_ref, state_ref):
    block_states(False, back_ref, got_ref, mine_ref, factor_ref, state_ref)


def my_block_kernel(
    back_ref, got_ref, mine_ref, factor_ref, wx_ref, wg_ref, bc_ref, state_ref, part_ref
):
    block_states(True, back_ref, got_ref, mine_ref, factor_ref, state_ref)
    part_ref[0] = half_sum(core(), state_ref, wx_ref, TOK, bc_ref[0])
    part_ref[1] = half_sum(core(), state_ref, wg_ref, 0, bc_ref[1])


def sums_kernel(other_ref, wx_ref, wg_ref, part_ref, send_hbm, sum_ref, sems):
    count = send_hbm.shape[0]
    copies = []
    for k, (weighted_ref, start) in enumerate(((wx_ref, TOK), (wg_ref, 0))):
        total = half_sum(1 - core(), other_ref, weighted_ref, start, part_ref[k])
        rows = pl.ds(k * TOK, TOK)
        sum_ref[rows, :] = total.astype(BF16)
        copies += load(
            [(sum_ref.at[rows], send_hbm.at[z, rows]) for z in range(count)], sems.at[k]
        )
    for copy in copies:
        copy.wait()


def grads_kernel(
    own_ref, other_ref, wx_ref, wg_ref, mats_ref, gx_ref, inner_ref, end_ref, out_ref, decay_ref
):
    b_mat = mats_ref[0]
    c_mat = mats_ref[1]
    last = iota(0) == TOK - 1
    alphas = jnp.zeros((TOK, LANES), F32)
    betas = jnp.zeros((TOK, LANES), F32)
    for half, state_ref in ((core(), own_ref), (1 - core(), other_ref)):
        for i in range(PAIRS // 2):
            lanes = half_pair(half, i)
            from_adjoint = nn(b_mat, state_ref[TOK : 2 * TOK, pair(i)])
            out_ref[:, lanes] = (gx_ref[:, lanes] + end_ref[:, lanes] * from_adjoint).astype(BF16)
            beta = wx_ref[:, lanes].astype(F32) * from_adjoint
            alpha = wg_ref[:, lanes].astype(F32) * nn(c_mat, state_ref[0:TOK, pair(i)])
            constant = one_row(state_ref[2 * TOK : 2 * TOK + TAIL, pair(i)])
            alpha = alpha + jnp.where(last, constant, 0.0)
            head = 2 * (half * (PAIRS // 2) + i)
            pick = (iota(1) == head + iota(0) // HALF).astype(BF16)
            beta_high, beta_low = split(beta)
            alpha_high, alpha_low = split(alpha)
            betas = betas + nn(beta_high, pick) + nn(beta_low, pick)
            alphas = alphas + nn(alpha_high, pick) + nn(alpha_low, pick)
    after = (iota(0) <= iota(1)).astype(F32)
    before = (iota(0) > iota(1)).astype(F32)
    decay = nn(after, alphas, HIGHEST) + nn(before, betas, HIGHEST)
    decay_ref[...] = inner_ref[...] + decay.T[0:HEADS, :]


def head_sum_kernel(parts_ref, b_ref, c_ref):
    b_ref[...] = jnp.sum(parts_ref[:, 0:TOK, :].astype(F32), axis=0).astype(BF16)
    c_ref[...] = jnp.sum(parts_ref[:, TOK : 2 * TOK, :].astype(F32), axis=0).astype(BF16)


HBM_SPEC = pl.BlockSpec(memory_space=pltpu.HBM)


def call(body, outs, micros, *args, from_hbm=False, to_hbm=False, scratch=()):
    more = {}
    if from_hbm:
        more["in_specs"] = [HBM_SPEC] * len(args)
        args = [pltpu.with_memory_space_constraint(a, pltpu.HBM) for a in args]
    if to_hbm:
        more["out_specs"] = [HBM_SPEC] * len(outs)
    return pl.pallas_call(
        body,
        out_shape=[jax.ShapeDtypeStruct(s, d) for s, d in outs],
        scratch_shapes=list(scratch),
        compiler_params=pltpu.CompilerParams(vmem_limit_bytes=24 * 1024 * 1024),
        cost_estimate=pl.CostEstimate(
            flops=int(micros * 1e9), bytes_accessed=1 << 18, transcendentals=0
        ),
        **more,
    )(*args)


def per_device(seq, heads, x, b_mat, c_mat, log_decay, grad):
    chips = seq // 2
    assert chips == PAIRS // 2 * CHUNKS
    inputs = (x, b_mat, c_mat, log_decay, grad)
    swap = [(i, i ^ 1) for i in range(seq)]
    same_core = [[2 * m + c for m in range(chips)] for c in range(2)]
    wide = (TOK, WIDE)
    half = (TOK, HALF_WIDE)
    states = (2 * TOK + TAIL, HALF_WIDE)
    slices_shape = (chips, SEND_TILES, 2, LANES)

    def loaded(shape):
        return (
            pltpu.VMEM(shape, BF16),
            pltpu.VMEM((TOK, LANES), BF16),
            pltpu.VMEM((TOK, LANES), BF16),
            pltpu.VMEM((HEADS, TOK), F32),
            pltpu.VMEM(shape, BF16),
        )

    spreads = (pltpu.VMEM(half, F32), pltpu.VMEM(half, F32))
    square = ((TOK, LANES), BF16)
    send, *for_mine = call(
        their_states_kernel,
        [(states, BF16), (half, BF16), (half, BF16), ((TOK, HEADS // 2), F32), square, square],
        1,
        *inputs,
        from_hbm=True,
        scratch=loaded(half) + spreads + (pltpu.SemaphoreType.DMA((7,)),),
    )
    got = lax.ppermute(send, "seq", swap)
    mine, factor = call(
        my_states_kernel,
        [((2 * TOK, HALF_WIDE), F32), ((8, HALF_WIDE), F32)],
        1,
        *for_mine,
        scratch=spreads,
    )
    (send,) = call(
        chip_kernel,
        [(slices_shape, BF16)],
        1,
        got,
        mine,
        factor,
        to_hbm=True,
        scratch=(pltpu.VMEM(slices_shape, BF16), pltpu.SemaphoreType.DMA((PAIRS // 2,))),
    )
    gathered = lax.all_to_all(send, "seq", 0, 0, tiled=True, axis_index_groups=same_core)
    local = call(
        intra_kernel,
        [
            (wide, F32),
            ((HEADS, TOK), F32),
            ((2, TOK, LANES), F32),
            (wide, BF16),
            (wide, BF16),
            ((2, TOK, LANES), BF16),
            (wide, F32),
        ],
        3,
        *inputs,
        from_hbm=True,
        scratch=loaded(wide) + (pltpu.SemaphoreType.DMA((5,)),),
    )
    gathered, (gx, inner, bc, wx, wg, mats, end) = lax.optimization_barrier((gathered, local))
    (back,) = call(recurrence_kernel, [(slices_shape, BF16)], 1, gathered)
    back = lax.all_to_all(back, "seq", 0, 0, tiled=True, axis_index_groups=same_core)
    (send,) = call(their_block_kernel, [(states, BF16)], 1, back, got, mine, factor)
    other = lax.ppermute(send, "seq", swap)
    own, part = call(
        my_block_kernel,
        [(states, BF16), ((2, TOK, LANES), F32)],
        1, back, got, mine, factor, wx, wg, bc,
    )
    (parts,) = call(
        sums_kernel,
        [((heads, 2 * TOK, LANES), BF16)],
        1,
        other,
        wx,
        wg,
        part,
        to_hbm=True,
        scratch=(pltpu.VMEM((2 * TOK, LANES), BF16), pltpu.SemaphoreType.DMA((2, heads))),
    )
    parts = lax.all_to_all(parts, "head", 0, 0, tiled=True)
    grad_x, decay_grad = call(
        grads_kernel,
        [(wide, BF16), ((HEADS, TOK), F32)],
        3,
        own, other, wx, wg, mats, gx, inner, end,
    )
    parts, grad_x, decay_grad = lax.optimization_barrier((parts, grad_x, decay_grad))
    grad_b, grad_c = call(head_sum_kernel, [((TOK, LANES), BF16)] * 2, 1, parts)
    return grad_x, grad_b, grad_c, decay_grad


def solution(mesh):
    in_specs = (
        P("seq", "head"),
        P("seq", None),
        P("seq", None),
        P("head", "seq"),
        P("seq", "head"),
    )
    out_specs = (P("seq", "head"), P("seq", None), P("seq", None), P("head", "seq"))
    return jax.shard_map(
        functools.partial(per_device, mesh.shape["seq"], mesh.shape["head"]),
        mesh=mesh,
        in_specs=in_specs,
        out_specs=out_specs,
        check_vma=False,
    )
```

```python
import functools

import jax
import jax.numpy as jnp
from jax import lax
from jax.experimental import pallas as pl
from jax.experimental.pallas import tpu as pltpu
from jax.sharding import PartitionSpec as P

F32 = jnp.float32
BF16 = jnp.bfloat16
HIGHEST = lax.Precision.HIGHEST
TOK = 128
LANES = 128
HALF = 64
HEADS = 16
WIDE = HEADS * HALF
HALF_WIDE = WIDE // 2
PAIRS = 8
CHUNKS = 8
ROWS = 16
SEND_ROWS = 2 * ROWS + 2
SEND_TILES = SEND_ROWS // 2
LEAD = 20
TAIL = 16


def nn(a, b, precision=None):
    return lax.dot_general(
        a, b, (((1,), (0,)), ((), ())), precision=precision, preferred_element_type=F32
    )


def nt(a, b, precision=None):
    return lax.dot_general(
        a, b, (((1,), (1,)), ((), ())), precision=precision, preferred_element_type=F32
    )


def iota(dim, shape=(TOK, LANES)):
    return lax.broadcasted_iota(jnp.int32, shape, dim)


def pair(g):
    return slice(g * LANES, (g + 1) * LANES)


def transposed(matrix):
    return matrix.astype(F32).T.astype(BF16)


def split(value):
    high = value.astype(BF16)
    return high, (value - high.astype(F32)).astype(BF16)


def cumulative_columns(log_decay):
    lower = (iota(0) >= iota(1)).astype(F32)
    return nt(lower, log_decay, HIGHEST)


def spread(columns, g):
    rows = columns.shape[0]
    left = iota(1, (rows, LANES)) < HALF
    a = jnp.broadcast_to(columns[:, 2 * g : 2 * g + 1], (rows, LANES))
    b = jnp.broadcast_to(columns[:, 2 * g + 1 : 2 * g + 2], (rows, LANES))
    return jnp.where(left, a, b)


def core():
    return lax.axis_index("seq") % 2


def first_core(shape):
    return jnp.full(shape, core(), jnp.int32) == 0


def half_lanes(half):
    return pl.ds(pl.multiple_of(half * HALF_WIDE, HALF_WIDE), HALF_WIDE)


def half_pair(half, i):
    return pl.ds(pl.multiple_of(half * HALF_WIDE + i * LANES, LANES), LANES)


def two_rows(value, rows):
    wide = jnp.broadcast_to(value, (rows, LANES))
    high = wide.astype(BF16).astype(F32)
    return jnp.where(iota(0, (rows, LANES)) == 0, high, wide - high).astype(BF16)


def one_row(rows):
    rows = rows.astype(F32)
    return rows[0:1, :] + rows[1:2, :]


def put(ref, k, rows):
    for j in range(SEND_TILES):
        ref[k, j] = rows[2 * j : 2 * j + 2]


def take(ref, k):
    return ref[k].reshape(SEND_ROWS, LANES)


def load(pairs, sems):
    copies = [pltpu.make_async_copy(a, b, sems.at[i]) for i, (a, b) in enumerate(pairs)]
    for copy in copies:
        copy.start()
    return copies


def states_of_half(cum, b_t, c_t, x_ref, grad_ref, end_ref, start_ref, copies=()):
    total = cum[TOK - 1 : TOK, :]
    to_end = jnp.exp(total - cum)
    from_start = jnp.exp(cum)
    last = jnp.exp(total)
    for i in range(PAIRS // 2):
        end_ref[:, pair(i)] = spread(to_end, i)
        start_ref[:, pair(i)] = spread(from_start, i)
    for copy in copies:
        copy.wait()
    for i in range(PAIRS // 2):
        wx = (x_ref[:, pair(i)].astype(F32) * end_ref[:, pair(i)]).astype(BF16)
        wg = (grad_ref[:, pair(i)].astype(F32) * start_ref[:, pair(i)]).astype(BF16)
        yield i, nn(b_t, wx), nn(c_t, wg), spread(last, i)


def their_states_kernel(
    x_hbm, b_hbm, c_hbm, log_hbm, grad_hbm,
    send_ref, x_mine, grad_mine, cum_mine, b_t_ref, c_t_ref,
    x_ref, b_ref, c_ref, log_ref, grad_ref, end_ref, start_ref, sems,
):
    theirs = half_lanes(1 - core())
    mine = half_lanes(core())
    copies = load(
        [
            (log_hbm, log_ref),
            (b_hbm, b_ref),
            (c_hbm, c_ref),
            (x_hbm.at[:, theirs], x_ref),
            (grad_hbm.at[:, theirs], grad_ref),
            (x_hbm.at[:, mine], x_mine),
            (grad_hbm.at[:, mine], grad_mine),
        ],
        sems,
    )
    copies[0].wait()
    both = cumulative_columns(log_ref[...])
    lower, upper = both[:, 0 : HEADS // 2], both[:, HEADS // 2 :]
    lower_mine = first_core((TOK, HEADS // 2))
    cum_mine[...] = jnp.where(lower_mine, lower, upper)
    copies[1].wait()
    b_t = transposed(b_ref[...])
    b_t_ref[...] = b_t
    copies[2].wait()
    c_t = transposed(c_ref[...])
    c_t_ref[...] = c_t
    for i, ends, opens, factor in states_of_half(
        jnp.where(lower_mine, upper, lower),
        b_t, c_t, x_ref, grad_ref, end_ref, start_ref, copies[3:5],
    ):
        send_ref[0:TOK, pair(i)] = ends.astype(BF16)
        send_ref[TOK : 2 * TOK, pair(i)] = opens.astype(BF16)
        send_ref[2 * TOK : 2 * TOK + TAIL, pair(i)] = two_rows(factor, TAIL)
    copies[5].wait()
    copies[6].wait()


def my_states_kernel(
    x_ref, grad_ref, cum_ref, b_t_ref, c_t_ref, mine_ref, factor_ref, end_ref, start_ref
):
    for i, ends, opens, factor in states_of_half(
        cum_ref[...], b_t_ref[...], c_t_ref[...], x_ref, grad_ref, end_ref, start_ref
    ):
        mine_ref[0:TOK, pair(i)] = ends
        mine_ref[TOK : 2 * TOK, pair(i)] = opens
        factor_ref[:, pair(i)] = jnp.broadcast_to(factor, (8, LANES))


def chip_kernel(got_ref, mine_ref, factor_ref, send_hbm, send_ref, sems):
    first = first_core((TOK, LANES))
    first_row = first_core((1, LANES))
    copies = []
    for i in range(PAIRS // 2):
        mine = factor_ref[0:1, pair(i)]
        theirs = one_row(got_ref[2 * TOK : 2 * TOK + TAIL, pair(i)])
        factor0 = jnp.where(first_row, mine, theirs)
        factor1 = jnp.where(first_row, theirs, mine)
        my_ends = mine_ref[0:TOK, pair(i)]
        my_opens = mine_ref[TOK : 2 * TOK, pair(i)]
        ends = got_ref[0:TOK, pair(i)].astype(F32)
        opens = got_ref[TOK : 2 * TOK, pair(i)].astype(F32)
        chip_ends = factor1 * jnp.where(first, my_ends, ends) + jnp.where(first, ends, my_ends)
        chip_opens = factor0 * jnp.where(first, opens, my_opens) + jnp.where(first, my_opens, opens)
        chip_ends = chip_ends.astype(BF16)
        chip_opens = chip_opens.astype(BF16)
        factors = two_rows(mine * theirs, 2)
        for r in range(CHUNKS):
            rows = slice(r * ROWS, (r + 1) * ROWS)
            block = jnp.concatenate([chip_ends[rows], chip_opens[rows], factors], axis=0)
            put(send_ref, i * CHUNKS + r, block)
        owners = pl.ds(i * CHUNKS, CHUNKS)
        copies.append(pltpu.make_async_copy(send_ref.at[owners], send_hbm.at[owners], sems.at[i]))
        copies[i].start()
    for copy in copies:
        copy.wait()


def recurrence_kernel(lead, got_ref, back_ref):
    count = got_ref.shape[0]
    entry = jnp.zeros((ROWS, LANES), F32)
    adjoint = jnp.zeros((ROWS, LANES), F32)
    place = [(k - lead) % count for k in range(count)]
    blocks = [take(got_ref, place[k]) for k in range(count)]
    entries, adjoints = [None] * count, [None] * count
    for k in range(count):
        m = count - 1 - k
        entries[k], adjoints[m] = entry, adjoint
        entry = one_row(blocks[k][2 * ROWS :]) * entry + blocks[k][0:ROWS].astype(F32)
        adjoint = one_row(blocks[m][2 * ROWS :]) * adjoint + blocks[m][ROWS : 2 * ROWS].astype(F32)
    for k in range(count):
        overlap = jnp.sum(entries[k] * adjoints[k], axis=0, keepdims=True)
        block = [entries[k].astype(BF16), adjoints[k].astype(BF16), two_rows(overlap, 2)]
        put(back_ref, place[k], jnp.concatenate(block, axis=0))


def intra_kernel(
    x_hbm, b_hbm, c_hbm, log_hbm, grad_hbm,
    gx_ref, decay_ref, bc_ref, wx_ref, wg_ref, mats_ref, end_ref,
    x_ref, b_ref, c_ref, log_ref, grad_ref, sems,
):
    copies = load(
        [(log_hbm, log_ref), (b_hbm, b_ref), (c_hbm, c_ref), (x_hbm, x_ref), (grad_hbm, grad_ref)],
        sems,
    )
    for copy in copies:
        copy.wait()
    log_decay = log_ref[...]
    upper = (iota(0) <= iota(1)).astype(F32)
    cum_rows = nn(log_decay, upper, HIGHEST)
    cum = cumulative_columns(log_decay)
    to_end = jnp.exp(cum[TOK - 1 : TOK, :] - cum)
    from_start = jnp.exp(cum)
    b_mat = b_ref[...]
    c_mat = c_ref[...]
    mats_ref[0] = b_mat
    mats_ref[1] = c_mat
    scores = nt(b_mat, c_mat)
    later = iota(1) >= iota(0)
    before = iota(0) < iota(1)
    ends_after = (iota(0) >= iota(1)).astype(BF16)
    left = iota(1) < HALF
    mixed_sum = jnp.zeros((TOK, TOK), F32)
    for g in range(PAIRS):
        x_g = x_ref[:, pair(g)]
        grad_g = grad_ref[:, pair(g)]
        end_g = spread(to_end, g)
        end_ref[:, pair(g)] = end_g
        wx_ref[:, pair(g)] = (x_g.astype(F32) * end_g).astype(BF16)
        wg_ref[:, pair(g)] = (grad_g.astype(F32) * spread(from_start, g)).astype(BF16)
        grad_x = jnp.zeros((TOK, LANES), F32)
        for j in range(2):
            h = 2 * g + j
            mine = left if j == 0 else jnp.logical_not(left)
            x_h = jnp.where(mine, x_g, jnp.zeros_like(x_g))
            grad_h = jnp.where(mine, grad_g, jnp.zeros_like(grad_g))
            pairs = nt(x_h, grad_g)
            gaps = cum_rows[h : h + 1, :] - cum[:, h : h + 1]
            decays = jnp.exp(jnp.where(later, gaps, -1e4))
            kernel = decays * scores
            mixed_sum = mixed_sum + decays * pairs
            grad_x = grad_x + nn(kernel.astype(BF16), grad_h)
            reach = nn((kernel * pairs).astype(BF16), ends_after)
            decay_ref[h : h + 1, :] = jnp.sum(
                jnp.where(before, reach, 0.0), axis=0, keepdims=True
            )
        gx_ref[:, pair(g)] = grad_x
    high, low = split(mixed_sum)
    high_t, low_t = split(mixed_sum.T)
    bc_ref[0] = nn(high, c_mat) + nn(low, c_mat)
    bc_ref[1] = nn(high_t, b_mat) + nn(low_t, b_mat)


def block_states(mine, back_ref, got_ref, mine_ref, factor_ref, out_ref):
    inside_is_adjoint = first_core((TOK, LANES)) == mine
    for i in range(PAIRS // 2):
        my_factor = factor_ref[0:1, pair(i)]
        their_factor = one_row(got_ref[2 * TOK : 2 * TOK + TAIL, pair(i)])
        blocks = [take(back_ref, i * CHUNKS + r) for r in range(CHUNKS)]
        entry = jnp.concatenate([block[0:ROWS] for block in blocks], axis=0).astype(F32)
        adjoint = jnp.concatenate([block[ROWS : 2 * ROWS] for block in blocks], axis=0).astype(F32)
        chip = sum(one_row(block[2 * ROWS :]) for block in blocks)
        if mine:
            opens = got_ref[TOK : 2 * TOK, pair(i)].astype(F32)
            ends = got_ref[0:TOK, pair(i)].astype(F32)
        else:
            opens = mine_ref[TOK : 2 * TOK, pair(i)]
            ends = mine_ref[0:TOK, pair(i)]
        beyond, here, added = (
            jnp.where(inside_is_adjoint, a, b)
            for a, b in ((adjoint, entry), (entry, adjoint), (opens, ends))
        )
        factor, block_factor = (
            (their_factor, my_factor) if mine else (my_factor, their_factor)
        )
        inside = factor * beyond + added
        constant = block_factor * (factor * chip + jnp.sum(here * added, axis=0, keepdims=True))
        out_ref[0:TOK, pair(i)] = jnp.where(inside_is_adjoint, here, inside).astype(BF16)
        out_ref[TOK : 2 * TOK, pair(i)] = jnp.where(inside_is_adjoint, inside, here).astype(BF16)
        out_ref[2 * TOK : 2 * TOK + TAIL, pair(i)] = two_rows(constant, TAIL)


def half_sum(half, state_ref, weighted_ref, start, total):
    for i in range(PAIRS // 2):
        total = total + nt(weighted_ref[:, half_pair(half, i)], state_ref[start : start + TOK, pair(i)])
    return total


def their_block_kernel(back_ref, got_ref, mine_ref, factor_ref, state_ref):
    block_states(False, back_ref, got_ref, mine_ref, factor_ref, state_ref)


def my_block_kernel(
    back_ref, got_ref, mine_ref, factor_ref, wx_ref, wg_ref, bc_ref, state_ref, part_ref
):
    block_states(True, back_ref, got_ref, mine_ref, factor_ref, state_ref)
    part_ref[0] = half_sum(core(), state_ref, wx_ref, TOK, bc_ref[0])
    part_ref[1] = half_sum(core(), state_ref, wg_ref, 0, bc_ref[1])


def sums_kernel(other_ref, wx_ref, wg_ref, part_ref, send_hbm, sum_ref, sems):
    count = send_hbm.shape[0]
    copies = []
    for k, (weighted_ref, start) in enumerate(((wx_ref, TOK), (wg_ref, 0))):
        total = half_sum(1 - core(), other_ref, weighted_ref, start, part_ref[k])
        rows = pl.ds(k * TOK, TOK)
        sum_ref[rows, :] = total.astype(BF16)
        copies += load(
            [(sum_ref.at[rows], send_hbm.at[z, rows]) for z in range(count)], sems.at[k]
        )
    for copy in copies:
        copy.wait()


def grads_kernel(
    own_ref, other_ref, wx_ref, wg_ref, mats_ref, gx_ref, inner_ref, end_ref, out_ref, decay_ref
):
    b_mat = mats_ref[0]
    c_mat = mats_ref[1]
    last = iota(0) == TOK - 1
    alphas = jnp.zeros((TOK, LANES), F32)
    betas = jnp.zeros((TOK, LANES), F32)
    for half, state_ref in ((core(), own_ref), (1 - core(), other_ref)):
        for i in range(PAIRS // 2):
            lanes = half_pair(half, i)
            from_adjoint = nn(b_mat, state_ref[TOK : 2 * TOK, pair(i)])
            out_ref[:, lanes] = (gx_ref[:, lanes] + end_ref[:, lanes] * from_adjoint).astype(BF16)
            beta = wx_ref[:, lanes].astype(F32) * from_adjoint
            alpha = wg_ref[:, lanes].astype(F32) * nn(c_mat, state_ref[0:TOK, pair(i)])
            constant = one_row(state_ref[2 * TOK : 2 * TOK + TAIL, pair(i)])
            alpha = alpha + jnp.where(last, constant, 0.0)
            head = 2 * (half * (PAIRS // 2) + i)
            pick = (iota(1) == head + iota(0) // HALF).astype(BF16)
            beta_high, beta_low = split(beta)
            alpha_high, alpha_low = split(alpha)
            betas = betas + nn(beta_high, pick) + nn(beta_low, pick)
            alphas = alphas + nn(alpha_high, pick) + nn(alpha_low, pick)
    after = (iota(0) <= iota(1)).astype(F32)
    before = (iota(0) > iota(1)).astype(F32)
    decay = nn(after, alphas, HIGHEST) + nn(before, betas, HIGHEST)
    decay_ref[...] = inner_ref[...] + decay.T[0:HEADS, :]


def head_sum_kernel(parts_ref, b_ref, c_ref):
    b_ref[...] = jnp.sum(parts_ref[:, 0:TOK, :].astype(F32), axis=0).astype(BF16)
    c_ref[...] = jnp.sum(parts_ref[:, TOK : 2 * TOK, :].astype(F32), axis=0).astype(BF16)


HBM_SPEC = pl.BlockSpec(memory_space=pltpu.HBM)


def call(body, outs, micros, *args, from_hbm=False, to_hbm=False, scratch=()):
    more = {}
    if from_hbm:
        more["in_specs"] = [HBM_SPEC] * len(args)
        args = [pltpu.with_memory_space_constraint(a, pltpu.HBM) for a in args]
    if to_hbm:
        more["out_specs"] = [HBM_SPEC] * len(outs)
    return pl.pallas_call(
        body,
        out_shape=[jax.ShapeDtypeStruct(s, d) for s, d in outs],
        scratch_shapes=list(scratch),
        compiler_params=pltpu.CompilerParams(vmem_limit_bytes=24 * 1024 * 1024),
        cost_estimate=pl.CostEstimate(
            flops=int(micros * 1e9), bytes_accessed=1 << 18, transcendentals=0
        ),
        **more,
    )(*args)


def per_device(seq, heads, x, b_mat, c_mat, log_decay, grad):
    chips = seq // 2
    assert chips == PAIRS // 2 * CHUNKS
    inputs = (x, b_mat, c_mat, log_decay, grad)
    swap = [(i, i ^ 1) for i in range(seq)]
    lead = LEAD
    same_core = [[2 * ((m + lead) % chips) + c for m in range(chips)] for c in range(2)]
    wide = (TOK, WIDE)
    half = (TOK, HALF_WIDE)
    states = (2 * TOK + TAIL, HALF_WIDE)
    slices_shape = (chips, SEND_TILES, 2, LANES)

    def loaded(shape):
        return (
            pltpu.VMEM(shape, BF16),
            pltpu.VMEM((TOK, LANES), BF16),
            pltpu.VMEM((TOK, LANES), BF16),
            pltpu.VMEM((HEADS, TOK), F32),
            pltpu.VMEM(shape, BF16),
        )

    spreads = (pltpu.VMEM(half, F32), pltpu.VMEM(half, F32))
    square = ((TOK, LANES), BF16)
    send, *for_mine = call(
        their_states_kernel,
        [(states, BF16), (half, BF16), (half, BF16), ((TOK, HEADS // 2), F32), square, square],
        1,
        *inputs,
        from_hbm=True,
        scratch=loaded(half) + spreads + (pltpu.SemaphoreType.DMA((7,)),),
    )
    got = lax.ppermute(send, "seq", swap)
    mine, factor = call(
        my_states_kernel,
        [((2 * TOK, HALF_WIDE), F32), ((8, HALF_WIDE), F32)],
        1,
        *for_mine,
        scratch=spreads,
    )
    (send,) = call(
        chip_kernel,
        [(slices_shape, BF16)],
        1,
        got,
        mine,
        factor,
        to_hbm=True,
        scratch=(pltpu.VMEM(slices_shape, BF16), pltpu.SemaphoreType.DMA((PAIRS // 2,))),
    )
    gathered = lax.all_to_all(send, "seq", 0, 0, tiled=True, axis_index_groups=same_core)
    local = call(
        intra_kernel,
        [
            (wide, F32),
            ((HEADS, TOK), F32),
            ((2, TOK, LANES), F32),
            (wide, BF16),
            (wide, BF16),
            ((2, TOK, LANES), BF16),
            (wide, F32),
        ],
        3,
        *inputs,
        from_hbm=True,
        scratch=loaded(wide) + (pltpu.SemaphoreType.DMA((5,)),),
    )
    gathered, (gx, inner, bc, wx, wg, mats, end) = lax.optimization_barrier((gathered, local))
    (back,) = call(functools.partial(recurrence_kernel, lead), [(slices_shape, BF16)], 1, gathered)
    back = lax.all_to_all(back, "seq", 0, 0, tiled=True, axis_index_groups=same_core)
    (send,) = call(their_block_kernel, [(states, BF16)], 1, back, got, mine, factor)
    other = lax.ppermute(send, "seq", swap)
    own, part = call(
        my_block_kernel,
        [(states, BF16), ((2, TOK, LANES), F32)],
        1, back, got, mine, factor, wx, wg, bc,
    )
    (parts,) = call(
        sums_kernel,
        [((heads, 2 * TOK, LANES), BF16)],
        1,
        other,
        wx,
        wg,
        part,
        to_hbm=True,
        scratch=(pltpu.VMEM((2 * TOK, LANES), BF16), pltpu.SemaphoreType.DMA((2, heads))),
    )
    parts = lax.all_to_all(parts, "head", 0, 0, tiled=True)
    grad_x, decay_grad = call(
        grads_kernel,
        [(wide, BF16), ((HEADS, TOK), F32)],
        3,
        own, other, wx, wg, mats, gx, inner, end,
    )
    parts, grad_x, decay_grad = lax.optimization_barrier((parts, grad_x, decay_grad))
    grad_b, grad_c = call(head_sum_kernel, [((TOK, LANES), BF16)] * 2, 1, parts)
    return grad_x, grad_b, grad_c, decay_grad


def solution(mesh):
    in_specs = (
        P("seq", "head"),
        P("seq", None),
        P("seq", None),
        P("head", "seq"),
        P("seq", "head"),
    )
    out_specs = (P("seq", "head"), P("seq", None), P("seq", None), P("head", "seq"))
    return jax.shard_map(
        functools.partial(per_device, mesh.shape["seq"], mesh.shape["head"]),
        mesh=mesh,
        in_specs=in_specs,
        out_specs=out_specs,
        check_vma=False,
    )
```

```python
import functools

import jax
import jax.numpy as jnp
from jax import lax
from jax.experimental import pallas as pl
from jax.experimental.pallas import tpu as pltpu
from jax.sharding import PartitionSpec as P

F32 = jnp.float32
BF16 = jnp.bfloat16
HIGHEST = lax.Precision.HIGHEST
TOK = 128
LANES = 128
HALF = 64
HEADS = 16
WIDE = HEADS * HALF
HALF_WIDE = WIDE // 2
PAIRS = 8
CHUNKS = 8
ROWS = 16
SEND_ROWS = 2 * ROWS + 2
SEND_TILES = SEND_ROWS // 2
LEAD = 20
TAIL = 16


def nn(a, b, precision=None):
    return lax.dot_general(
        a, b, (((1,), (0,)), ((), ())), precision=precision, preferred_element_type=F32
    )


def nt(a, b, precision=None):
    return lax.dot_general(
        a, b, (((1,), (1,)), ((), ())), precision=precision, preferred_element_type=F32
    )


def iota(dim, shape=(TOK, LANES)):
    return lax.broadcasted_iota(jnp.int32, shape, dim)


def pair(g):
    return slice(g * LANES, (g + 1) * LANES)


def transposed(matrix):
    return matrix.astype(F32).T.astype(BF16)


def split(value):
    high = value.astype(BF16)
    return high, (value - high.astype(F32)).astype(BF16)


def cumulative_columns(log_decay):
    lower = (iota(0) >= iota(1)).astype(F32)
    return nt(lower, log_decay, HIGHEST)


def spread(columns, g):
    rows = columns.shape[0]
    left = iota(1, (rows, LANES)) < HALF
    a = jnp.broadcast_to(columns[:, 2 * g : 2 * g + 1], (rows, LANES))
    b = jnp.broadcast_to(columns[:, 2 * g + 1 : 2 * g + 2], (rows, LANES))
    return jnp.where(left, a, b)


def core():
    return lax.axis_index("seq") % 2


def first_core(shape):
    return jnp.full(shape, core(), jnp.int32) == 0


def half_lanes(half):
    return pl.ds(pl.multiple_of(half * HALF_WIDE, HALF_WIDE), HALF_WIDE)


def half_pair(half, i):
    return pl.ds(pl.multiple_of(half * HALF_WIDE + i * LANES, LANES), LANES)


def two_rows(value, rows):
    wide = jnp.broadcast_to(value, (rows, LANES))
    high = wide.astype(BF16).astype(F32)
    return jnp.where(iota(0, (rows, LANES)) == 0, high, wide - high).astype(BF16)


def one_row(rows):
    rows = rows.astype(F32)
    return rows[0:1, :] + rows[1:2, :]


def put(ref, k, rows):
    for j in range(SEND_TILES):
        ref[k, j] = rows[2 * j : 2 * j + 2]


def take(ref, k):
    return ref[k].reshape(SEND_ROWS, LANES)


def load(pairs, sems):
    copies = [pltpu.make_async_copy(a, b, sems.at[i]) for i, (a, b) in enumerate(pairs)]
    for copy in copies:
        copy.start()
    return copies


def states_of_half(cum, b_t, c_t, x_ref, grad_ref, end_ref, start_ref, copies=()):
    total = cum[TOK - 1 : TOK, :]
    to_end = jnp.exp(total - cum)
    from_start = jnp.exp(cum)
    last = jnp.exp(total)
    for i in range(PAIRS // 2):
        end_ref[:, pair(i)] = spread(to_end, i)
        start_ref[:, pair(i)] = spread(from_start, i)
    for copy in copies:
        copy.wait()
    for i in range(PAIRS // 2):
        wx = (x_ref[:, pair(i)].astype(F32) * end_ref[:, pair(i)]).astype(BF16)
        wg = (grad_ref[:, pair(i)].astype(F32) * start_ref[:, pair(i)]).astype(BF16)
        yield i, nn(b_t, wx), nn(c_t, wg), spread(last, i)


def their_states_kernel(
    x_hbm, b_hbm, c_hbm, log_hbm, grad_hbm,
    send_ref, x_mine, grad_mine, cum_mine, b_t_ref, c_t_ref,
    x_ref, b_ref, c_ref, log_ref, grad_ref, end_ref, start_ref, sems,
):
    theirs = half_lanes(1 - core())
    mine = half_lanes(core())
    copies = load(
        [
            (log_hbm, log_ref),
            (b_hbm, b_ref),
            (c_hbm, c_ref),
            (x_hbm.at[:, theirs], x_ref),
            (grad_hbm.at[:, theirs], grad_ref),
            (x_hbm.at[:, mine], x_mine),
            (grad_hbm.at[:, mine], grad_mine),
        ],
        sems,
    )
    copies[0].wait()
    both = cumulative_columns(log_ref[...])
    lower, upper = both[:, 0 : HEADS // 2], both[:, HEADS // 2 :]
    lower_mine = first_core((TOK, HEADS // 2))
    cum_mine[...] = jnp.where(lower_mine, lower, upper)
    copies[1].wait()
    b_t = transposed(b_ref[...])
    b_t_ref[...] = b_t
    copies[2].wait()
    c_t = transposed(c_ref[...])
    c_t_ref[...] = c_t
    for i, ends, opens, factor in states_of_half(
        jnp.where(lower_mine, upper, lower),
        b_t, c_t, x_ref, grad_ref, end_ref, start_ref, copies[3:5],
    ):
        send_ref[0:TOK, pair(i)] = ends.astype(BF16)
        send_ref[TOK : 2 * TOK, pair(i)] = opens.astype(BF16)
        send_ref[2 * TOK : 2 * TOK + TAIL, pair(i)] = two_rows(factor, TAIL)
    copies[5].wait()
    copies[6].wait()


def my_states_kernel(
    x_ref, grad_ref, cum_ref, b_t_ref, c_t_ref, mine_ref, factor_ref, end_ref, start_ref
):
    for i, ends, opens, factor in states_of_half(
        cum_ref[...], b_t_ref[...], c_t_ref[...], x_ref, grad_ref, end_ref, start_ref
    ):
        mine_ref[0:TOK, pair(i)] = ends
        mine_ref[TOK : 2 * TOK, pair(i)] = opens
        factor_ref[:, pair(i)] = jnp.broadcast_to(factor, (8, LANES))


def chip_kernel(got_ref, mine_ref, factor_ref, send_hbm, send_ref, sems):
    first = first_core((TOK, LANES))
    first_row = first_core((1, LANES))
    copies = []
    for i in range(PAIRS // 2):
        mine = factor_ref[0:1, pair(i)]
        theirs = one_row(got_ref[2 * TOK : 2 * TOK + TAIL, pair(i)])
        factor0 = jnp.where(first_row, mine, theirs)
        factor1 = jnp.where(first_row, theirs, mine)
        my_ends = mine_ref[0:TOK, pair(i)]
        my_opens = mine_ref[TOK : 2 * TOK, pair(i)]
        ends = got_ref[0:TOK, pair(i)].astype(F32)
        opens = got_ref[TOK : 2 * TOK, pair(i)].astype(F32)
        chip_ends = factor1 * jnp.where(first, my_ends, ends) + jnp.where(first, ends, my_ends)
        chip_opens = factor0 * jnp.where(first, opens, my_opens) + jnp.where(first, my_opens, opens)
        chip_ends = chip_ends.astype(BF16)
        chip_opens = chip_opens.astype(BF16)
        factors = two_rows(mine * theirs, 2)
        for r in range(CHUNKS):
            rows = slice(r * ROWS, (r + 1) * ROWS)
            block = jnp.concatenate([chip_ends[rows], chip_opens[rows], factors], axis=0)
            put(send_ref, i * CHUNKS + r, block)
        owners = pl.ds(i * CHUNKS, CHUNKS)
        copies.append(pltpu.make_async_copy(send_ref.at[owners], send_hbm.at[owners], sems.at[i]))
        copies[i].start()
    for copy in copies:
        copy.wait()


def recurrence_kernel(lead, got_ref, back_ref):
    count = got_ref.shape[0]
    entry = jnp.zeros((ROWS, LANES), F32)
    adjoint = jnp.zeros((ROWS, LANES), F32)
    place = [(k - lead) % count for k in range(count)]
    blocks = [take(got_ref, place[k]) for k in range(count)]
    entries, adjoints = [None] * count, [None] * count
    for k in range(count):
        m = count - 1 - k
        entries[k], adjoints[m] = entry, adjoint
        entry = one_row(blocks[k][2 * ROWS :]) * entry + blocks[k][0:ROWS].astype(F32)
        adjoint = one_row(blocks[m][2 * ROWS :]) * adjoint + blocks[m][ROWS : 2 * ROWS].astype(F32)
    for k in range(count):
        overlap = jnp.sum(entries[k] * adjoints[k], axis=0, keepdims=True)
        block = [entries[k].astype(BF16), adjoints[k].astype(BF16), two_rows(overlap, 2)]
        put(back_ref, place[k], jnp.concatenate(block, axis=0))


def intra_kernel(
    x_hbm, b_hbm, c_hbm, log_hbm, grad_hbm,
    gx_ref, decay_ref, bc_ref, wx_ref, wg_ref, mats_ref, end_ref,
    x_ref, b_ref, c_ref, log_ref, grad_ref, sems,
):
    copies = load(
        [(log_hbm, log_ref), (b_hbm, b_ref), (c_hbm, c_ref), (x_hbm, x_ref), (grad_hbm, grad_ref)],
        sems,
    )
    for copy in copies:
        copy.wait()
    log_decay = log_ref[...]
    upper = (iota(0) <= iota(1)).astype(F32)
    cum_rows = nn(log_decay, upper, HIGHEST)
    cum = cumulative_columns(log_decay)
    to_end = jnp.exp(cum[TOK - 1 : TOK, :] - cum)
    from_start = jnp.exp(cum)
    b_mat = b_ref[...]
    c_mat = c_ref[...]
    mats_ref[0] = b_mat
    mats_ref[1] = c_mat
    scores = nt(b_mat, c_mat)
    later = iota(1) >= iota(0)
    before = iota(0) < iota(1)
    ends_after = (iota(0) >= iota(1)).astype(BF16)
    left = iota(1) < HALF
    mixed_sum = jnp.zeros((TOK, TOK), F32)
    for g in range(PAIRS):
        x_g = x_ref[:, pair(g)]
        grad_g = grad_ref[:, pair(g)]
        end_g = spread(to_end, g)
        end_ref[:, pair(g)] = end_g
        wx_ref[:, pair(g)] = (x_g.astype(F32) * end_g).astype(BF16)
        wg_ref[:, pair(g)] = (grad_g.astype(F32) * spread(from_start, g)).astype(BF16)
        grad_x = jnp.zeros((TOK, LANES), F32)
        for j in range(2):
            h = 2 * g + j
            mine = left if j == 0 else jnp.logical_not(left)
            x_h = jnp.where(mine, x_g, jnp.zeros_like(x_g))
            grad_h = jnp.where(mine, grad_g, jnp.zeros_like(grad_g))
            pairs = nt(x_h, grad_g)
            gaps = cum_rows[h : h + 1, :] - cum[:, h : h + 1]
            decays = jnp.exp(jnp.where(later, gaps, -1e4))
            kernel = decays * scores
            mixed_sum = mixed_sum + decays * pairs
            grad_x = grad_x + nn(kernel.astype(BF16), grad_h)
            reach = nn((kernel * pairs).astype(BF16), ends_after)
            decay_ref[h : h + 1, :] = jnp.sum(
                jnp.where(before, reach, 0.0), axis=0, keepdims=True
            )
        gx_ref[:, pair(g)] = grad_x
    high, low = split(mixed_sum)
    high_t, low_t = split(mixed_sum.T)
    bc_ref[0] = nn(high, c_mat) + nn(low, c_mat)
    bc_ref[1] = nn(high_t, b_mat) + nn(low_t, b_mat)


def block_states(mine, back_ref, got_ref, mine_ref, factor_ref, out_ref):
    inside_is_adjoint = first_core((TOK, LANES)) == mine
    for i in range(PAIRS // 2):
        my_factor = factor_ref[0:1, pair(i)]
        their_factor = one_row(got_ref[2 * TOK : 2 * TOK + TAIL, pair(i)])
        blocks = [take(back_ref, i * CHUNKS + r) for r in range(CHUNKS)]
        entry = jnp.concatenate([block[0:ROWS] for block in blocks], axis=0).astype(F32)
        adjoint = jnp.concatenate([block[ROWS : 2 * ROWS] for block in blocks], axis=0).astype(F32)
        chip = sum(one_row(block[2 * ROWS :]) for block in blocks)
        if mine:
            opens = got_ref[TOK : 2 * TOK, pair(i)].astype(F32)
            ends = got_ref[0:TOK, pair(i)].astype(F32)
        else:
            opens = mine_ref[TOK : 2 * TOK, pair(i)]
            ends = mine_ref[0:TOK, pair(i)]
        beyond, here, added = (
            jnp.where(inside_is_adjoint, a, b)
            for a, b in ((adjoint, entry), (entry, adjoint), (opens, ends))
        )
        factor, block_factor = (
            (their_factor, my_factor) if mine else (my_factor, their_factor)
        )
        inside = factor * beyond + added
        constant = block_factor * (factor * chip + jnp.sum(here * added, axis=0, keepdims=True))
        out_ref[0:TOK, pair(i)] = jnp.where(inside_is_adjoint, here, inside).astype(BF16)
        out_ref[TOK : 2 * TOK, pair(i)] = jnp.where(inside_is_adjoint, inside, here).astype(BF16)
        out_ref[2 * TOK : 2 * TOK + TAIL, pair(i)] = two_rows(constant, TAIL)


def half_sum(half, state_ref, weighted_ref, start, total):
    for i in range(PAIRS // 2):
        total = total + nt(weighted_ref[:, half_pair(half, i)], state_ref[start : start + TOK, pair(i)])
    return total


def their_block_kernel(back_ref, got_ref, mine_ref, factor_ref, state_ref):
    block_states(False, back_ref, got_ref, mine_ref, factor_ref, state_ref)


def my_block_kernel(
    back_ref, got_ref, mine_ref, factor_ref, wx_ref, wg_ref, bc_ref, state_ref, part_ref
):
    block_states(True, back_ref, got_ref, mine_ref, factor_ref, state_ref)
    part_ref[0] = half_sum(core(), state_ref, wx_ref, TOK, bc_ref[0])
    part_ref[1] = half_sum(core(), state_ref, wg_ref, 0, bc_ref[1])


def sums_kernel(other_ref, wx_ref, wg_ref, part_ref, send_hbm, sum_ref, sems):
    count = send_hbm.shape[0]
    copies = []
    for k, (weighted_ref, start) in enumerate(((wx_ref, TOK), (wg_ref, 0))):
        total = half_sum(1 - core(), other_ref, weighted_ref, start, part_ref[k])
        rows = pl.ds(k * TOK, TOK)
        sum_ref[rows, :] = total.astype(BF16)
        copies += load(
            [(sum_ref.at[rows], send_hbm.at[z, rows]) for z in range(count)], sems.at[k]
        )
    for copy in copies:
        copy.wait()


def grads_kernel(
    own_ref, other_ref, wx_ref, wg_ref, mats_ref, gx_ref, inner_ref, end_ref, out_ref, decay_ref
):
    b_mat = mats_ref[0]
    c_mat = mats_ref[1]
    last = iota(0) == TOK - 1
    alphas = jnp.zeros((TOK, LANES), F32)
    betas = jnp.zeros((TOK, LANES), F32)
    for half, state_ref in ((core(), own_ref), (1 - core(), other_ref)):
        for i in range(PAIRS // 2):
            lanes = half_pair(half, i)
            from_adjoint = nn(b_mat, state_ref[TOK : 2 * TOK, pair(i)])
            out_ref[:, lanes] = (gx_ref[:, lanes] + end_ref[:, lanes] * from_adjoint).astype(BF16)
            beta = wx_ref[:, lanes].astype(F32) * from_adjoint
            alpha = wg_ref[:, lanes].astype(F32) * nn(c_mat, state_ref[0:TOK, pair(i)])
            constant = one_row(state_ref[2 * TOK : 2 * TOK + TAIL, pair(i)])
            alpha = alpha + jnp.where(last, constant, 0.0)
            head = 2 * (half * (PAIRS // 2) + i)
            pick = (iota(1) == head + iota(0) // HALF).astype(BF16)
            beta_high, beta_low = split(beta)
            alpha_high, alpha_low = split(alpha)
            betas = betas + nn(beta_high, pick) + nn(beta_low, pick)
            alphas = alphas + nn(alpha_high, pick) + nn(alpha_low, pick)
    after = (iota(0) <= iota(1)).astype(F32)
    before = (iota(0) > iota(1)).astype(F32)
    decay = nn(after, alphas, HIGHEST) + nn(before, betas, HIGHEST)
    decay_ref[...] = inner_ref[...] + decay.T[0:HEADS, :]


def head_sum_kernel(parts_ref, b_ref, c_ref):
    b_ref[...] = jnp.sum(parts_ref[:, 0:TOK, :].astype(F32), axis=0).astype(BF16)
    c_ref[...] = jnp.sum(parts_ref[:, TOK : 2 * TOK, :].astype(F32), axis=0).astype(BF16)


HBM_SPEC = pl.BlockSpec(memory_space=pltpu.HBM)


def call(body, outs, micros, *args, from_hbm=False, to_hbm=False, scratch=()):
    more = {}
    if from_hbm:
        more["in_specs"] = [HBM_SPEC] * len(args)
        args = [pltpu.with_memory_space_constraint(a, pltpu.HBM) for a in args]
    if to_hbm:
        more["out_specs"] = [HBM_SPEC] * len(outs)
    return pl.pallas_call(
        body,
        out_shape=[jax.ShapeDtypeStruct(s, d) for s, d in outs],
        scratch_shapes=list(scratch),
        compiler_params=pltpu.CompilerParams(vmem_limit_bytes=24 * 1024 * 1024),
        cost_estimate=pl.CostEstimate(
            flops=int(micros * 1e9), bytes_accessed=1 << 18, transcendentals=0
        ),
        **more,
    )(*args)


def per_device(seq, heads, x, b_mat, c_mat, log_decay, grad):
    chips = seq // 2
    assert chips == PAIRS // 2 * CHUNKS
    inputs = (x, b_mat, c_mat, log_decay, grad)
    swap = [(i, i ^ 1) for i in range(seq)]
    lead = LEAD
    same_core = [[2 * ((m + lead) % chips) + c for m in range(chips)] for c in range(2)]
    last_plane_first = [[(z + heads - 1) % heads for z in range(heads)]]
    wide = (TOK, WIDE)
    half = (TOK, HALF_WIDE)
    states = (2 * TOK + TAIL, HALF_WIDE)
    slices_shape = (chips, SEND_TILES, 2, LANES)

    def loaded(shape):
        return (
            pltpu.VMEM(shape, BF16),
            pltpu.VMEM((TOK, LANES), BF16),
            pltpu.VMEM((TOK, LANES), BF16),
            pltpu.VMEM((HEADS, TOK), F32),
            pltpu.VMEM(shape, BF16),
        )

    spreads = (pltpu.VMEM(half, F32), pltpu.VMEM(half, F32))
    square = ((TOK, LANES), BF16)
    send, *for_mine = call(
        their_states_kernel,
        [(states, BF16), (half, BF16), (half, BF16), ((TOK, HEADS // 2), F32), square, square],
        1,
        *inputs,
        from_hbm=True,
        scratch=loaded(half) + spreads + (pltpu.SemaphoreType.DMA((7,)),),
    )
    got = lax.ppermute(send, "seq", swap)
    mine, factor = call(
        my_states_kernel,
        [((2 * TOK, HALF_WIDE), F32), ((8, HALF_WIDE), F32)],
        1,
        *for_mine,
        scratch=spreads,
    )
    (send,) = call(
        chip_kernel,
        [(slices_shape, BF16)],
        1,
        got,
        mine,
        factor,
        to_hbm=True,
        scratch=(pltpu.VMEM(slices_shape, BF16), pltpu.SemaphoreType.DMA((PAIRS // 2,))),
    )
    gathered = lax.all_to_all(send, "seq", 0, 0, tiled=True, axis_index_groups=same_core)
    local = call(
        intra_kernel,
        [
            (wide, F32),
            ((HEADS, TOK), F32),
            ((2, TOK, LANES), F32),
            (wide, BF16),
            (wide, BF16),
            ((2, TOK, LANES), BF16),
            (wide, F32),
        ],
        3,
        *inputs,
        from_hbm=True,
        scratch=loaded(wide) + (pltpu.SemaphoreType.DMA((5,)),),
    )
    gathered, (gx, inner, bc, wx, wg, mats, end) = lax.optimization_barrier((gathered, local))
    (back,) = call(functools.partial(recurrence_kernel, lead), [(slices_shape, BF16)], 1, gathered)
    back = lax.all_to_all(back, "seq", 0, 0, tiled=True, axis_index_groups=same_core)
    (send,) = call(their_block_kernel, [(states, BF16)], 1, back, got, mine, factor)
    other = lax.ppermute(send, "seq", swap)
    own, part = call(
        my_block_kernel,
        [(states, BF16), ((2, TOK, LANES), F32)],
        1, back, got, mine, factor, wx, wg, bc,
    )
    (parts,) = call(
        sums_kernel,
        [((heads, 2 * TOK, LANES), BF16)],
        1,
        other,
        wx,
        wg,
        part,
        to_hbm=True,
        scratch=(pltpu.VMEM((2 * TOK, LANES), BF16), pltpu.SemaphoreType.DMA((2, heads))),
    )
    parts = lax.all_to_all(parts, "head", 0, 0, tiled=True, axis_index_groups=last_plane_first)
    grad_x, decay_grad = call(
        grads_kernel,
        [(wide, BF16), ((HEADS, TOK), F32)],
        3,
        own, other, wx, wg, mats, gx, inner, end,
    )
    parts, grad_x, decay_grad = lax.optimization_barrier((parts, grad_x, decay_grad))
    grad_b, grad_c = call(head_sum_kernel, [((TOK, LANES), BF16)] * 2, 1, parts)
    return grad_x, grad_b, grad_c, decay_grad


def solution(mesh):
    in_specs = (
        P("seq", "head"),
        P("seq", None),
        P("seq", None),
        P("head", "seq"),
        P("seq", "head"),
    )
    out_specs = (P("seq", "head"), P("seq", None), P("seq", None), P("head", "seq"))
    return jax.shard_map(
        functools.partial(per_device, mesh.shape["seq"], mesh.shape["head"]),
        mesh=mesh,
        in_specs=in_specs,
        out_specs=out_specs,
        check_vma=False,
    )
```

```python
import functools

import jax
import jax.numpy as jnp
from jax import lax
from jax.experimental import pallas as pl
from jax.experimental.pallas import tpu as pltpu
from jax.sharding import PartitionSpec as P

F32 = jnp.float32
BF16 = jnp.bfloat16
HIGHEST = lax.Precision.HIGHEST
TOK = 128
LANES = 128
HALF = 64
HEADS = 16
WIDE = HEADS * HALF
HALF_WIDE = WIDE // 2
PAIRS = 8
CHUNKS = 8
ROWS = 16
SEND_ROWS = 2 * ROWS + 2
SEND_TILES = SEND_ROWS // 2
LAST_CHIP = 20
CHIP_STRIDE = 11
PLANE_STRIDE = 3
TAIL = 16


def nn(a, b, precision=None):
    return lax.dot_general(
        a, b, (((1,), (0,)), ((), ())), precision=precision, preferred_element_type=F32
    )


def nt(a, b, precision=None):
    return lax.dot_general(
        a, b, (((1,), (1,)), ((), ())), precision=precision, preferred_element_type=F32
    )


def iota(dim, shape=(TOK, LANES)):
    return lax.broadcasted_iota(jnp.int32, shape, dim)


def pair(g):
    return slice(g * LANES, (g + 1) * LANES)


def transposed(matrix):
    return matrix.astype(F32).T.astype(BF16)


def split(value):
    high = value.astype(BF16)
    return high, (value - high.astype(F32)).astype(BF16)


def cumulative_columns(log_decay):
    lower = (iota(0) >= iota(1)).astype(F32)
    return nt(lower, log_decay, HIGHEST)


def spread(columns, g):
    rows = columns.shape[0]
    left = iota(1, (rows, LANES)) < HALF
    a = jnp.broadcast_to(columns[:, 2 * g : 2 * g + 1], (rows, LANES))
    b = jnp.broadcast_to(columns[:, 2 * g + 1 : 2 * g + 2], (rows, LANES))
    return jnp.where(left, a, b)


def core():
    return lax.axis_index("seq") % 2


def first_core(shape):
    return jnp.full(shape, core(), jnp.int32) == 0


def half_lanes(half):
    return pl.ds(pl.multiple_of(half * HALF_WIDE, HALF_WIDE), HALF_WIDE)


def half_pair(half, i):
    return pl.ds(pl.multiple_of(half * HALF_WIDE + i * LANES, LANES), LANES)


def two_rows(value, rows):
    wide = jnp.broadcast_to(value, (rows, LANES))
    high = wide.astype(BF16).astype(F32)
    return jnp.where(iota(0, (rows, LANES)) == 0, high, wide - high).astype(BF16)


def one_row(rows):
    rows = rows.astype(F32)
    return rows[0:1, :] + rows[1:2, :]


def put(ref, k, rows):
    for j in range(SEND_TILES):
        ref[k, j] = rows[2 * j : 2 * j + 2]


def take(ref, k):
    return ref[k].reshape(SEND_ROWS, LANES)


def load(pairs, sems):
    copies = [pltpu.make_async_copy(a, b, sems.at[i]) for i, (a, b) in enumerate(pairs)]
    for copy in copies:
        copy.start()
    return copies


def states_of_half(cum, b_t, c_t, x_ref, grad_ref, end_ref, start_ref, copies=()):
    total = cum[TOK - 1 : TOK, :]
    to_end = jnp.exp(total - cum)
    from_start = jnp.exp(cum)
    last = jnp.exp(total)
    for i in range(PAIRS // 2):
        end_ref[:, pair(i)] = spread(to_end, i)
        start_ref[:, pair(i)] = spread(from_start, i)
    for copy in copies:
        copy.wait()
    for i in range(PAIRS // 2):
        wx = (x_ref[:, pair(i)].astype(F32) * end_ref[:, pair(i)]).astype(BF16)
        wg = (grad_ref[:, pair(i)].astype(F32) * start_ref[:, pair(i)]).astype(BF16)
        yield i, nn(b_t, wx), nn(c_t, wg), spread(last, i)


def their_states_kernel(
    x_hbm, b_hbm, c_hbm, log_hbm, grad_hbm,
    send_ref, x_mine, grad_mine, cum_mine, b_t_ref, c_t_ref,
    x_ref, b_ref, c_ref, log_ref, grad_ref, end_ref, start_ref, sems,
):
    theirs = half_lanes(1 - core())
    mine = half_lanes(core())
    copies = load(
        [
            (log_hbm, log_ref),
            (b_hbm, b_ref),
            (c_hbm, c_ref),
            (x_hbm.at[:, theirs], x_ref),
            (grad_hbm.at[:, theirs], grad_ref),
            (x_hbm.at[:, mine], x_mine),
            (grad_hbm.at[:, mine], grad_mine),
        ],
        sems,
    )
    copies[0].wait()
    both = cumulative_columns(log_ref[...])
    lower, upper = both[:, 0 : HEADS // 2], both[:, HEADS // 2 :]
    lower_mine = first_core((TOK, HEADS // 2))
    cum_mine[...] = jnp.where(lower_mine, lower, upper)
    copies[1].wait()
    b_t = transposed(b_ref[...])
    b_t_ref[...] = b_t
    copies[2].wait()
    c_t = transposed(c_ref[...])
    c_t_ref[...] = c_t
    for i, ends, opens, factor in states_of_half(
        jnp.where(lower_mine, upper, lower),
        b_t, c_t, x_ref, grad_ref, end_ref, start_ref, copies[3:5],
    ):
        send_ref[0:TOK, pair(i)] = ends.astype(BF16)
        send_ref[TOK : 2 * TOK, pair(i)] = opens.astype(BF16)
        send_ref[2 * TOK : 2 * TOK + TAIL, pair(i)] = two_rows(factor, TAIL)
    copies[5].wait()
    copies[6].wait()


def my_states_kernel(
    x_ref, grad_ref, cum_ref, b_t_ref, c_t_ref, mine_ref, factor_ref, end_ref, start_ref
):
    for i, ends, opens, factor in states_of_half(
        cum_ref[...], b_t_ref[...], c_t_ref[...], x_ref, grad_ref, end_ref, start_ref
    ):
        mine_ref[0:TOK, pair(i)] = ends
        mine_ref[TOK : 2 * TOK, pair(i)] = opens
        factor_ref[:, pair(i)] = jnp.broadcast_to(factor, (8, LANES))


def chip_kernel(got_ref, mine_ref, factor_ref, send_hbm, send_ref, sems):
    first = first_core((TOK, LANES))
    first_row = first_core((1, LANES))
    copies = []
    for i in range(PAIRS // 2):
        mine = factor_ref[0:1, pair(i)]
        theirs = one_row(got_ref[2 * TOK : 2 * TOK + TAIL, pair(i)])
        factor0 = jnp.where(first_row, mine, theirs)
        factor1 = jnp.where(first_row, theirs, mine)
        my_ends = mine_ref[0:TOK, pair(i)]
        my_opens = mine_ref[TOK : 2 * TOK, pair(i)]
        ends = got_ref[0:TOK, pair(i)].astype(F32)
        opens = got_ref[TOK : 2 * TOK, pair(i)].astype(F32)
        chip_ends = factor1 * jnp.where(first, my_ends, ends) + jnp.where(first, ends, my_ends)
        chip_opens = factor0 * jnp.where(first, opens, my_opens) + jnp.where(first, my_opens, opens)
        chip_ends = chip_ends.astype(BF16)
        chip_opens = chip_opens.astype(BF16)
        factors = two_rows(mine * theirs, 2)
        for r in range(CHUNKS):
            rows = slice(r * ROWS, (r + 1) * ROWS)
            block = jnp.concatenate([chip_ends[rows], chip_opens[rows], factors], axis=0)
            put(send_ref, i * CHUNKS + r, block)
        owners = pl.ds(i * CHUNKS, CHUNKS)
        copies.append(pltpu.make_async_copy(send_ref.at[owners], send_hbm.at[owners], sems.at[i]))
        copies[i].start()
    for copy in copies:
        copy.wait()


def recurrence_kernel(place, got_ref, back_ref):
    count = got_ref.shape[0]
    entry = jnp.zeros((ROWS, LANES), F32)
    adjoint = jnp.zeros((ROWS, LANES), F32)
    blocks = [take(got_ref, place[k]) for k in range(count)]
    entries, adjoints = [None] * count, [None] * count
    for k in range(count):
        m = count - 1 - k
        entries[k], adjoints[m] = entry, adjoint
        entry = one_row(blocks[k][2 * ROWS :]) * entry + blocks[k][0:ROWS].astype(F32)
        adjoint = one_row(blocks[m][2 * ROWS :]) * adjoint + blocks[m][ROWS : 2 * ROWS].astype(F32)
    for k in range(count):
        overlap = jnp.sum(entries[k] * adjoints[k], axis=0, keepdims=True)
        block = [entries[k].astype(BF16), adjoints[k].astype(BF16), two_rows(overlap, 2)]
        put(back_ref, place[k], jnp.concatenate(block, axis=0))


def intra_kernel(
    x_hbm, b_hbm, c_hbm, log_hbm, grad_hbm,
    gx_ref, decay_ref, bc_ref, wx_ref, wg_ref, mats_ref, end_ref,
    x_ref, b_ref, c_ref, log_ref, grad_ref, sems,
):
    copies = load(
        [(log_hbm, log_ref), (b_hbm, b_ref), (c_hbm, c_ref), (x_hbm, x_ref), (grad_hbm, grad_ref)],
        sems,
    )
    for copy in copies:
        copy.wait()
    log_decay = log_ref[...]
    upper = (iota(0) <= iota(1)).astype(F32)
    cum_rows = nn(log_decay, upper, HIGHEST)
    cum = cumulative_columns(log_decay)
    to_end = jnp.exp(cum[TOK - 1 : TOK, :] - cum)
    from_start = jnp.exp(cum)
    b_mat = b_ref[...]
    c_mat = c_ref[...]
    mats_ref[0] = b_mat
    mats_ref[1] = c_mat
    scores = nt(b_mat, c_mat)
    later = iota(1) >= iota(0)
    before = iota(0) < iota(1)
    ends_after = (iota(0) >= iota(1)).astype(BF16)
    left = iota(1) < HALF
    mixed_sum = jnp.zeros((TOK, TOK), F32)
    for g in range(PAIRS):
        x_g = x_ref[:, pair(g)]
        grad_g = grad_ref[:, pair(g)]
        end_g = spread(to_end, g)
        end_ref[:, pair(g)] = end_g
        wx_ref[:, pair(g)] = (x_g.astype(F32) * end_g).astype(BF16)
        wg_ref[:, pair(g)] = (grad_g.astype(F32) * spread(from_start, g)).astype(BF16)
        grad_x = jnp.zeros((TOK, LANES), F32)
        for j in range(2):
            h = 2 * g + j
            mine = left if j == 0 else jnp.logical_not(left)
            x_h = jnp.where(mine, x_g, jnp.zeros_like(x_g))
            grad_h = jnp.where(mine, grad_g, jnp.zeros_like(grad_g))
            pairs = nt(x_h, grad_g)
            gaps = cum_rows[h : h + 1, :] - cum[:, h : h + 1]
            decays = jnp.exp(jnp.where(later, gaps, -1e4))
            kernel = decays * scores
            mixed_sum = mixed_sum + decays * pairs
            grad_x = grad_x + nn(kernel.astype(BF16), grad_h)
            reach = nn((kernel * pairs).astype(BF16), ends_after)
            decay_ref[h : h + 1, :] = jnp.sum(
                jnp.where(before, reach, 0.0), axis=0, keepdims=True
            )
        gx_ref[:, pair(g)] = grad_x
    high, low = split(mixed_sum)
    high_t, low_t = split(mixed_sum.T)
    bc_ref[0] = nn(high, c_mat) + nn(low, c_mat)
    bc_ref[1] = nn(high_t, b_mat) + nn(low_t, b_mat)


def block_states(mine, back_ref, got_ref, mine_ref, factor_ref, out_ref):
    inside_is_adjoint = first_core((TOK, LANES)) == mine
    for i in range(PAIRS // 2):
        my_factor = factor_ref[0:1, pair(i)]
        their_factor = one_row(got_ref[2 * TOK : 2 * TOK + TAIL, pair(i)])
        blocks = [take(back_ref, i * CHUNKS + r) for r in range(CHUNKS)]
        entry = jnp.concatenate([block[0:ROWS] for block in blocks], axis=0).astype(F32)
        adjoint = jnp.concatenate([block[ROWS : 2 * ROWS] for block in blocks], axis=0).astype(F32)
        chip = sum(one_row(block[2 * ROWS :]) for block in blocks)
        if mine:
            opens = got_ref[TOK : 2 * TOK, pair(i)].astype(F32)
            ends = got_ref[0:TOK, pair(i)].astype(F32)
        else:
            opens = mine_ref[TOK : 2 * TOK, pair(i)]
            ends = mine_ref[0:TOK, pair(i)]
        beyond, here, added = (
            jnp.where(inside_is_adjoint, a, b)
            for a, b in ((adjoint, entry), (entry, adjoint), (opens, ends))
        )
        factor, block_factor = (
            (their_factor, my_factor) if mine else (my_factor, their_factor)
        )
        inside = factor * beyond + added
        constant = block_factor * (factor * chip + jnp.sum(here * added, axis=0, keepdims=True))
        out_ref[0:TOK, pair(i)] = jnp.where(inside_is_adjoint, here, inside).astype(BF16)
        out_ref[TOK : 2 * TOK, pair(i)] = jnp.where(inside_is_adjoint, inside, here).astype(BF16)
        out_ref[2 * TOK : 2 * TOK + TAIL, pair(i)] = two_rows(constant, TAIL)


def half_sum(half, state_ref, weighted_ref, start, total):
    for i in range(PAIRS // 2):
        total = total + nt(weighted_ref[:, half_pair(half, i)], state_ref[start : start + TOK, pair(i)])
    return total


def their_block_kernel(back_ref, got_ref, mine_ref, factor_ref, state_ref):
    block_states(False, back_ref, got_ref, mine_ref, factor_ref, state_ref)


def my_block_kernel(
    back_ref, got_ref, mine_ref, factor_ref, wx_ref, wg_ref, bc_ref, state_ref, part_ref
):
    block_states(True, back_ref, got_ref, mine_ref, factor_ref, state_ref)
    part_ref[0] = half_sum(core(), state_ref, wx_ref, TOK, bc_ref[0])
    part_ref[1] = half_sum(core(), state_ref, wg_ref, 0, bc_ref[1])


def sums_kernel(other_ref, wx_ref, wg_ref, part_ref, send_hbm, sum_ref, sems):
    count = send_hbm.shape[0]
    copies = []
    for k, (weighted_ref, start) in enumerate(((wx_ref, TOK), (wg_ref, 0))):
        total = half_sum(1 - core(), other_ref, weighted_ref, start, part_ref[k])
        rows = pl.ds(k * TOK, TOK)
        sum_ref[rows, :] = total.astype(BF16)
        copies += load(
            [(sum_ref.at[rows], send_hbm.at[z, rows]) for z in range(count)], sems.at[k]
        )
    for copy in copies:
        copy.wait()


def grads_kernel(
    own_ref, other_ref, wx_ref, wg_ref, mats_ref, gx_ref, inner_ref, end_ref, out_ref, decay_ref
):
    b_mat = mats_ref[0]
    c_mat = mats_ref[1]
    last = iota(0) == TOK - 1
    alphas = jnp.zeros((TOK, LANES), F32)
    betas = jnp.zeros((TOK, LANES), F32)
    for half, state_ref in ((core(), own_ref), (1 - core(), other_ref)):
        for i in range(PAIRS // 2):
            lanes = half_pair(half, i)
            from_adjoint = nn(b_mat, state_ref[TOK : 2 * TOK, pair(i)])
            out_ref[:, lanes] = (gx_ref[:, lanes] + end_ref[:, lanes] * from_adjoint).astype(BF16)
            beta = wx_ref[:, lanes].astype(F32) * from_adjoint
            alpha = wg_ref[:, lanes].astype(F32) * nn(c_mat, state_ref[0:TOK, pair(i)])
            constant = one_row(state_ref[2 * TOK : 2 * TOK + TAIL, pair(i)])
            alpha = alpha + jnp.where(last, constant, 0.0)
            head = 2 * (half * (PAIRS // 2) + i)
            pick = (iota(1) == head + iota(0) // HALF).astype(BF16)
            beta_high, beta_low = split(beta)
            alpha_high, alpha_low = split(alpha)
            betas = betas + nn(beta_high, pick) + nn(beta_low, pick)
            alphas = alphas + nn(alpha_high, pick) + nn(alpha_low, pick)
    after = (iota(0) <= iota(1)).astype(F32)
    before = (iota(0) > iota(1)).astype(F32)
    decay = nn(after, alphas, HIGHEST) + nn(before, betas, HIGHEST)
    decay_ref[...] = inner_ref[...] + decay.T[0:HEADS, :]


def head_sum_kernel(parts_ref, b_ref, c_ref):
    b_ref[...] = jnp.sum(parts_ref[:, 0:TOK, :].astype(F32), axis=0).astype(BF16)
    c_ref[...] = jnp.sum(parts_ref[:, TOK : 2 * TOK, :].astype(F32), axis=0).astype(BF16)


HBM_SPEC = pl.BlockSpec(memory_space=pltpu.HBM)


def call(body, outs, micros, *args, from_hbm=False, to_hbm=False, scratch=()):
    more = {}
    if from_hbm:
        more["in_specs"] = [HBM_SPEC] * len(args)
        args = [pltpu.with_memory_space_constraint(a, pltpu.HBM) for a in args]
    if to_hbm:
        more["out_specs"] = [HBM_SPEC] * len(outs)
    return pl.pallas_call(
        body,
        out_shape=[jax.ShapeDtypeStruct(s, d) for s, d in outs],
        scratch_shapes=list(scratch),
        compiler_params=pltpu.CompilerParams(vmem_limit_bytes=24 * 1024 * 1024),
        cost_estimate=pl.CostEstimate(
            flops=int(micros * 1e9), bytes_accessed=1 << 18, transcendentals=0
        ),
        **more,
    )(*args)


def per_device(seq, heads, x, b_mat, c_mat, log_decay, grad):
    chips = seq // 2
    assert chips == PAIRS // 2 * CHUNKS
    inputs = (x, b_mat, c_mat, log_decay, grad)
    swap = [(i, i ^ 1) for i in range(seq)]
    order = [(LAST_CHIP + CHIP_STRIDE * i) % chips for i in range(chips)]
    place = [order.index(m) for m in range(chips)]
    same_core = [[2 * m + c for m in order] for c in range(2)]
    planes = [[(heads - 1 + PLANE_STRIDE * i) % heads for i in range(heads)]]
    wide = (TOK, WIDE)
    half = (TOK, HALF_WIDE)
    states = (2 * TOK + TAIL, HALF_WIDE)
    slices_shape = (chips, SEND_TILES, 2, LANES)

    def loaded(shape):
        return (
            pltpu.VMEM(shape, BF16),
            pltpu.VMEM((TOK, LANES), BF16),
            pltpu.VMEM((TOK, LANES), BF16),
            pltpu.VMEM((HEADS, TOK), F32),
            pltpu.VMEM(shape, BF16),
        )

    spreads = (pltpu.VMEM(half, F32), pltpu.VMEM(half, F32))
    square = ((TOK, LANES), BF16)
    send, *for_mine = call(
        their_states_kernel,
        [(states, BF16), (half, BF16), (half, BF16), ((TOK, HEADS // 2), F32), square, square],
        1,
        *inputs,
        from_hbm=True,
        scratch=loaded(half) + spreads + (pltpu.SemaphoreType.DMA((7,)),),
    )
    got = lax.ppermute(send, "seq", swap)
    mine, factor = call(
        my_states_kernel,
        [((2 * TOK, HALF_WIDE), F32), ((8, HALF_WIDE), F32)],
        1,
        *for_mine,
        scratch=spreads,
    )
    (send,) = call(
        chip_kernel,
        [(slices_shape, BF16)],
        1,
        got,
        mine,
        factor,
        to_hbm=True,
        scratch=(pltpu.VMEM(slices_shape, BF16), pltpu.SemaphoreType.DMA((PAIRS // 2,))),
    )
    gathered = lax.all_to_all(send, "seq", 0, 0, tiled=True, axis_index_groups=same_core)
    local = call(
        intra_kernel,
        [
            (wide, F32),
            ((HEADS, TOK), F32),
            ((2, TOK, LANES), F32),
            (wide, BF16),
            (wide, BF16),
            ((2, TOK, LANES), BF16),
            (wide, F32),
        ],
        3,
        *inputs,
        from_hbm=True,
        scratch=loaded(wide) + (pltpu.SemaphoreType.DMA((5,)),),
    )
    gathered, (gx, inner, bc, wx, wg, mats, end) = lax.optimization_barrier((gathered, local))
    (back,) = call(functools.partial(recurrence_kernel, place), [(slices_shape, BF16)], 1, gathered)
    back = lax.all_to_all(back, "seq", 0, 0, tiled=True, axis_index_groups=same_core)
    (send,) = call(their_block_kernel, [(states, BF16)], 1, back, got, mine, factor)
    other = lax.ppermute(send, "seq", swap)
    own, part = call(
        my_block_kernel,
        [(states, BF16), ((2, TOK, LANES), F32)],
        1, back, got, mine, factor, wx, wg, bc,
    )
    (parts,) = call(
        sums_kernel,
        [((heads, 2 * TOK, LANES), BF16)],
        1,
        other,
        wx,
        wg,
        part,
        to_hbm=True,
        scratch=(pltpu.VMEM((2 * TOK, LANES), BF16), pltpu.SemaphoreType.DMA((2, heads))),
    )
    parts = lax.all_to_all(parts, "head", 0, 0, tiled=True, axis_index_groups=planes)
    grad_x, decay_grad = call(
        grads_kernel,
        [(wide, BF16), ((HEADS, TOK), F32)],
        3,
        own, other, wx, wg, mats, gx, inner, end,
    )
    parts, grad_x, decay_grad = lax.optimization_barrier((parts, grad_x, decay_grad))
    grad_b, grad_c = call(head_sum_kernel, [((TOK, LANES), BF16)] * 2, 1, parts)
    return grad_x, grad_b, grad_c, decay_grad


def solution(mesh):
    in_specs = (
        P("seq", "head"),
        P("seq", None),
        P("seq", None),
        P("head", "seq"),
        P("seq", "head"),
    )
    out_specs = (P("seq", "head"), P("seq", None), P("seq", None), P("head", "seq"))
    return jax.shard_map(
        functools.partial(per_device, mesh.shape["seq"], mesh.shape["head"]),
        mesh=mesh,
        in_specs=in_specs,
        out_specs=out_specs,
        check_vma=False,
    )
```

```python
import functools

import jax
import jax.numpy as jnp
from jax import lax
from jax.experimental import pallas as pl
from jax.experimental.pallas import tpu as pltpu
from jax.sharding import PartitionSpec as P

F32 = jnp.float32
BF16 = jnp.bfloat16
HIGHEST = lax.Precision.HIGHEST
TOK = 128
LANES = 128
HALF = 64
HEADS = 16
WIDE = HEADS * HALF
HALF_WIDE = WIDE // 2
PAIRS = 8
CHUNKS = 8
ROWS = 16
SEND_ROWS = 2 * ROWS + 2
SEND_TILES = SEND_ROWS // 2
FIRST_CHIP = 20
FIRST_PLANE = 5
TAIL = 16


def nn(a, b, precision=None):
    return lax.dot_general(
        a, b, (((1,), (0,)), ((), ())), precision=precision, preferred_element_type=F32
    )


def nt(a, b, precision=None):
    return lax.dot_general(
        a, b, (((1,), (1,)), ((), ())), precision=precision, preferred_element_type=F32
    )


def iota(dim, shape=(TOK, LANES)):
    return lax.broadcasted_iota(jnp.int32, shape, dim)


def pair(g):
    return slice(g * LANES, (g + 1) * LANES)


def transposed(matrix):
    return matrix.astype(F32).T.astype(BF16)


def split(value):
    high = value.astype(BF16)
    return high, (value - high.astype(F32)).astype(BF16)


def cumulative_columns(log_decay):
    lower = (iota(0) >= iota(1)).astype(F32)
    return nt(lower, log_decay, HIGHEST)


def spread(columns, g):
    rows = columns.shape[0]
    left = iota(1, (rows, LANES)) < HALF
    a = jnp.broadcast_to(columns[:, 2 * g : 2 * g + 1], (rows, LANES))
    b = jnp.broadcast_to(columns[:, 2 * g + 1 : 2 * g + 2], (rows, LANES))
    return jnp.where(left, a, b)


def core():
    return lax.axis_index("seq") % 2


def first_core(shape):
    return jnp.full(shape, core(), jnp.int32) == 0


def half_lanes(half):
    return pl.ds(pl.multiple_of(half * HALF_WIDE, HALF_WIDE), HALF_WIDE)


def half_pair(half, i):
    return pl.ds(pl.multiple_of(half * HALF_WIDE + i * LANES, LANES), LANES)


def two_rows(value, rows):
    wide = jnp.broadcast_to(value, (rows, LANES))
    high = wide.astype(BF16).astype(F32)
    return jnp.where(iota(0, (rows, LANES)) == 0, high, wide - high).astype(BF16)


def one_row(rows):
    rows = rows.astype(F32)
    return rows[0:1, :] + rows[1:2, :]


def put(ref, k, rows):
    for j in range(SEND_TILES):
        ref[k, j] = rows[2 * j : 2 * j + 2]


def take(ref, k):
    return ref[k].reshape(SEND_ROWS, LANES)


def load(pairs, sems):
    copies = [pltpu.make_async_copy(a, b, sems.at[i]) for i, (a, b) in enumerate(pairs)]
    for copy in copies:
        copy.start()
    return copies


def states_of_half(cum, b_t, c_t, x_ref, grad_ref, end_ref, start_ref, copies=()):
    total = cum[TOK - 1 : TOK, :]
    to_end = jnp.exp(total - cum)
    from_start = jnp.exp(cum)
    last = jnp.exp(total)
    for i in range(PAIRS // 2):
        end_ref[:, pair(i)] = spread(to_end, i)
        start_ref[:, pair(i)] = spread(from_start, i)
    for copy in copies:
        copy.wait()
    for i in range(PAIRS // 2):
        wx = (x_ref[:, pair(i)].astype(F32) * end_ref[:, pair(i)]).astype(BF16)
        wg = (grad_ref[:, pair(i)].astype(F32) * start_ref[:, pair(i)]).astype(BF16)
        yield i, nn(b_t, wx), nn(c_t, wg), spread(last, i)


def their_states_kernel(
    x_hbm, b_hbm, c_hbm, log_hbm, grad_hbm,
    send_ref, x_mine, grad_mine, cum_mine, b_t_ref, c_t_ref,
    x_ref, b_ref, c_ref, log_ref, grad_ref, end_ref, start_ref, sems,
):
    theirs = half_lanes(1 - core())
    mine = half_lanes(core())
    copies = load(
        [
            (log_hbm, log_ref),
            (b_hbm, b_ref),
            (c_hbm, c_ref),
            (x_hbm.at[:, theirs], x_ref),
            (grad_hbm.at[:, theirs], grad_ref),
            (x_hbm.at[:, mine], x_mine),
            (grad_hbm.at[:, mine], grad_mine),
        ],
        sems,
    )
    copies[0].wait()
    both = cumulative_columns(log_ref[...])
    lower, upper = both[:, 0 : HEADS // 2], both[:, HEADS // 2 :]
    lower_mine = first_core((TOK, HEADS // 2))
    cum_mine[...] = jnp.where(lower_mine, lower, upper)
    copies[1].wait()
    b_t = transposed(b_ref[...])
    b_t_ref[...] = b_t
    copies[2].wait()
    c_t = transposed(c_ref[...])
    c_t_ref[...] = c_t
    for i, ends, opens, factor in states_of_half(
        jnp.where(lower_mine, upper, lower),
        b_t, c_t, x_ref, grad_ref, end_ref, start_ref, copies[3:5],
    ):
        send_ref[0:TOK, pair(i)] = ends.astype(BF16)
        send_ref[TOK : 2 * TOK, pair(i)] = opens.astype(BF16)
        send_ref[2 * TOK : 2 * TOK + TAIL, pair(i)] = two_rows(factor, TAIL)
    copies[5].wait()
    copies[6].wait()


def my_states_kernel(
    x_ref, grad_ref, cum_ref, b_t_ref, c_t_ref, mine_ref, factor_ref, end_ref, start_ref
):
    for i, ends, opens, factor in states_of_half(
        cum_ref[...], b_t_ref[...], c_t_ref[...], x_ref, grad_ref, end_ref, start_ref
    ):
        mine_ref[0:TOK, pair(i)] = ends
        mine_ref[TOK : 2 * TOK, pair(i)] = opens
        factor_ref[:, pair(i)] = jnp.broadcast_to(factor, (8, LANES))


def chip_kernel(got_ref, mine_ref, factor_ref, send_hbm, send_ref, sems):
    first = first_core((TOK, LANES))
    first_row = first_core((1, LANES))
    copies = []
    for i in range(PAIRS // 2):
        mine = factor_ref[0:1, pair(i)]
        theirs = one_row(got_ref[2 * TOK : 2 * TOK + TAIL, pair(i)])
        factor0 = jnp.where(first_row, mine, theirs)
        factor1 = jnp.where(first_row, theirs, mine)
        my_ends = mine_ref[0:TOK, pair(i)]
        my_opens = mine_ref[TOK : 2 * TOK, pair(i)]
        ends = got_ref[0:TOK, pair(i)].astype(F32)
        opens = got_ref[TOK : 2 * TOK, pair(i)].astype(F32)
        chip_ends = factor1 * jnp.where(first, my_ends, ends) + jnp.where(first, ends, my_ends)
        chip_opens = factor0 * jnp.where(first, opens, my_opens) + jnp.where(first, my_opens, opens)
        chip_ends = chip_ends.astype(BF16)
        chip_opens = chip_opens.astype(BF16)
        factors = two_rows(mine * theirs, 2)
        for r in range(CHUNKS):
            rows = slice(r * ROWS, (r + 1) * ROWS)
            block = jnp.concatenate([chip_ends[rows], chip_opens[rows], factors], axis=0)
            put(send_ref, i * CHUNKS + r, block)
        owners = pl.ds(i * CHUNKS, CHUNKS)
        copies.append(pltpu.make_async_copy(send_ref.at[owners], send_hbm.at[owners], sems.at[i]))
        copies[i].start()
    for copy in copies:
        copy.wait()


def recurrence_kernel(place, got_ref, back_ref):
    count = got_ref.shape[0]
    entry = jnp.zeros((ROWS, LANES), F32)
    adjoint = jnp.zeros((ROWS, LANES), F32)
    blocks = [take(got_ref, place[k]) for k in range(count)]
    entries, adjoints = [None] * count, [None] * count
    for k in range(count):
        m = count - 1 - k
        entries[k], adjoints[m] = entry, adjoint
        entry = one_row(blocks[k][2 * ROWS :]) * entry + blocks[k][0:ROWS].astype(F32)
        adjoint = one_row(blocks[m][2 * ROWS :]) * adjoint + blocks[m][ROWS : 2 * ROWS].astype(F32)
    for k in range(count):
        overlap = jnp.sum(entries[k] * adjoints[k], axis=0, keepdims=True)
        block = [entries[k].astype(BF16), adjoints[k].astype(BF16), two_rows(overlap, 2)]
        put(back_ref, place[k], jnp.concatenate(block, axis=0))


def intra_kernel(
    x_hbm, b_hbm, c_hbm, log_hbm, grad_hbm,
    gx_ref, decay_ref, bc_ref, wx_ref, wg_ref, mats_ref, end_ref,
    x_ref, b_ref, c_ref, log_ref, grad_ref, sems,
):
    copies = load(
        [(log_hbm, log_ref), (b_hbm, b_ref), (c_hbm, c_ref), (x_hbm, x_ref), (grad_hbm, grad_ref)],
        sems,
    )
    for copy in copies:
        copy.wait()
    log_decay = log_ref[...]
    upper = (iota(0) <= iota(1)).astype(F32)
    cum_rows = nn(log_decay, upper, HIGHEST)
    cum = cumulative_columns(log_decay)
    to_end = jnp.exp(cum[TOK - 1 : TOK, :] - cum)
    from_start = jnp.exp(cum)
    b_mat = b_ref[...]
    c_mat = c_ref[...]
    mats_ref[0] = b_mat
    mats_ref[1] = c_mat
    scores = nt(b_mat, c_mat)
    later = iota(1) >= iota(0)
    before = iota(0) < iota(1)
    ends_after = (iota(0) >= iota(1)).astype(BF16)
    left = iota(1) < HALF
    mixed_sum = jnp.zeros((TOK, TOK), F32)
    for g in range(PAIRS):
        x_g = x_ref[:, pair(g)]
        grad_g = grad_ref[:, pair(g)]
        end_g = spread(to_end, g)
        end_ref[:, pair(g)] = end_g
        wx_ref[:, pair(g)] = (x_g.astype(F32) * end_g).astype(BF16)
        wg_ref[:, pair(g)] = (grad_g.astype(F32) * spread(from_start, g)).astype(BF16)
        grad_x = jnp.zeros((TOK, LANES), F32)
        for j in range(2):
            h = 2 * g + j
            mine = left if j == 0 else jnp.logical_not(left)
            x_h = jnp.where(mine, x_g, jnp.zeros_like(x_g))
            grad_h = jnp.where(mine, grad_g, jnp.zeros_like(grad_g))
            pairs = nt(x_h, grad_g)
            gaps = cum_rows[h : h + 1, :] - cum[:, h : h + 1]
            decays = jnp.exp(jnp.where(later, gaps, -1e4))
            kernel = decays * scores
            mixed_sum = mixed_sum + decays * pairs
            grad_x = grad_x + nn(kernel.astype(BF16), grad_h)
            reach = nn((kernel * pairs).astype(BF16), ends_after)
            decay_ref[h : h + 1, :] = jnp.sum(
                jnp.where(before, reach, 0.0), axis=0, keepdims=True
            )
        gx_ref[:, pair(g)] = grad_x
    high, low = split(mixed_sum)
    high_t, low_t = split(mixed_sum.T)
    bc_ref[0] = nn(high, c_mat) + nn(low, c_mat)
    bc_ref[1] = nn(high_t, b_mat) + nn(low_t, b_mat)


def block_states(mine, back_ref, got_ref, mine_ref, factor_ref, out_ref):
    inside_is_adjoint = first_core((TOK, LANES)) == mine
    for i in range(PAIRS // 2):
        my_factor = factor_ref[0:1, pair(i)]
        their_factor = one_row(got_ref[2 * TOK : 2 * TOK + TAIL, pair(i)])
        blocks = [take(back_ref, i * CHUNKS + r) for r in range(CHUNKS)]
        entry = jnp.concatenate([block[0:ROWS] for block in blocks], axis=0).astype(F32)
        adjoint = jnp.concatenate([block[ROWS : 2 * ROWS] for block in blocks], axis=0).astype(F32)
        chip = sum(one_row(block[2 * ROWS :]) for block in blocks)
        if mine:
            opens = got_ref[TOK : 2 * TOK, pair(i)].astype(F32)
            ends = got_ref[0:TOK, pair(i)].astype(F32)
        else:
            opens = mine_ref[TOK : 2 * TOK, pair(i)]
            ends = mine_ref[0:TOK, pair(i)]
        beyond, here, added = (
            jnp.where(inside_is_adjoint, a, b)
            for a, b in ((adjoint, entry), (entry, adjoint), (opens, ends))
        )
        factor, block_factor = (
            (their_factor, my_factor) if mine else (my_factor, their_factor)
        )
        inside = factor * beyond + added
        constant = block_factor * (factor * chip + jnp.sum(here * added, axis=0, keepdims=True))
        out_ref[0:TOK, pair(i)] = jnp.where(inside_is_adjoint, here, inside).astype(BF16)
        out_ref[TOK : 2 * TOK, pair(i)] = jnp.where(inside_is_adjoint, inside, here).astype(BF16)
        out_ref[2 * TOK : 2 * TOK + TAIL, pair(i)] = two_rows(constant, TAIL)


def half_sum(half, state_ref, weighted_ref, start, total):
    for i in range(PAIRS // 2):
        total = total + nt(weighted_ref[:, half_pair(half, i)], state_ref[start : start + TOK, pair(i)])
    return total


def their_block_kernel(back_ref, got_ref, mine_ref, factor_ref, state_ref):
    block_states(False, back_ref, got_ref, mine_ref, factor_ref, state_ref)


def my_block_kernel(
    back_ref, got_ref, mine_ref, factor_ref, wx_ref, wg_ref, bc_ref, state_ref, part_ref
):
    block_states(True, back_ref, got_ref, mine_ref, factor_ref, state_ref)
    part_ref[0] = half_sum(core(), state_ref, wx_ref, TOK, bc_ref[0])
    part_ref[1] = half_sum(core(), state_ref, wg_ref, 0, bc_ref[1])


def sums_kernel(other_ref, wx_ref, wg_ref, part_ref, send_hbm, sum_ref, sems):
    count = send_hbm.shape[0]
    copies = []
    for k, (weighted_ref, start) in enumerate(((wx_ref, TOK), (wg_ref, 0))):
        total = half_sum(1 - core(), other_ref, weighted_ref, start, part_ref[k])
        rows = pl.ds(k * TOK, TOK)
        sum_ref[rows, :] = total.astype(BF16)
        copies += load(
            [(sum_ref.at[rows], send_hbm.at[z, rows]) for z in range(count)], sems.at[k]
        )
    for copy in copies:
        copy.wait()


def grads_kernel(
    own_ref, other_ref, wx_ref, wg_ref, mats_ref, gx_ref, inner_ref, end_ref, out_ref, decay_ref
):
    b_mat = mats_ref[0]
    c_mat = mats_ref[1]
    last = iota(0) == TOK - 1
    alphas = jnp.zeros((TOK, LANES), F32)
    betas = jnp.zeros((TOK, LANES), F32)
    for half, state_ref in ((core(), own_ref), (1 - core(), other_ref)):
        for i in range(PAIRS // 2):
            lanes = half_pair(half, i)
            from_adjoint = nn(b_mat, state_ref[TOK : 2 * TOK, pair(i)])
            out_ref[:, lanes] = (gx_ref[:, lanes] + end_ref[:, lanes] * from_adjoint).astype(BF16)
            beta = wx_ref[:, lanes].astype(F32) * from_adjoint
            alpha = wg_ref[:, lanes].astype(F32) * nn(c_mat, state_ref[0:TOK, pair(i)])
            constant = one_row(state_ref[2 * TOK : 2 * TOK + TAIL, pair(i)])
            alpha = alpha + jnp.where(last, constant, 0.0)
            head = 2 * (half * (PAIRS // 2) + i)
            pick = (iota(1) == head + iota(0) // HALF).astype(BF16)
            beta_high, beta_low = split(beta)
            alpha_high, alpha_low = split(alpha)
            betas = betas + nn(beta_high, pick) + nn(beta_low, pick)
            alphas = alphas + nn(alpha_high, pick) + nn(alpha_low, pick)
    after = (iota(0) <= iota(1)).astype(F32)
    before = (iota(0) > iota(1)).astype(F32)
    decay = nn(after, alphas, HIGHEST) + nn(before, betas, HIGHEST)
    decay_ref[...] = inner_ref[...] + decay.T[0:HEADS, :]


def head_sum_kernel(parts_ref, b_ref, c_ref):
    b_ref[...] = jnp.sum(parts_ref[:, 0:TOK, :].astype(F32), axis=0).astype(BF16)
    c_ref[...] = jnp.sum(parts_ref[:, TOK : 2 * TOK, :].astype(F32), axis=0).astype(BF16)


HBM_SPEC = pl.BlockSpec(memory_space=pltpu.HBM)


def call(body, outs, micros, *args, from_hbm=False, to_hbm=False, scratch=()):
    more = {}
    if from_hbm:
        more["in_specs"] = [HBM_SPEC] * len(args)
        args = [pltpu.with_memory_space_constraint(a, pltpu.HBM) for a in args]
    if to_hbm:
        more["out_specs"] = [HBM_SPEC] * len(outs)
    return pl.pallas_call(
        body,
        out_shape=[jax.ShapeDtypeStruct(s, d) for s, d in outs],
        scratch_shapes=list(scratch),
        compiler_params=pltpu.CompilerParams(vmem_limit_bytes=24 * 1024 * 1024),
        cost_estimate=pl.CostEstimate(
            flops=int(micros * 1e9), bytes_accessed=1 << 18, transcendentals=0
        ),
        **more,
    )(*args)


def per_device(seq, heads, x, b_mat, c_mat, log_decay, grad):
    chips = seq // 2
    assert chips == PAIRS // 2 * CHUNKS
    inputs = (x, b_mat, c_mat, log_decay, grad)
    swap = [(i, i ^ 1) for i in range(seq)]
    order = [(FIRST_CHIP + i) % chips for i in range(chips)]
    place = [order.index(m) for m in range(chips)]
    same_core = [[2 * m + c for m in order] for c in range(2)]
    planes = [[(FIRST_PLANE - i) % heads for i in range(heads)]]
    wide = (TOK, WIDE)
    half = (TOK, HALF_WIDE)
    states = (2 * TOK + TAIL, HALF_WIDE)
    slices_shape = (chips, SEND_TILES, 2, LANES)

    def loaded(shape):
        return (
            pltpu.VMEM(shape, BF16),
            pltpu.VMEM((TOK, LANES), BF16),
            pltpu.VMEM((TOK, LANES), BF16),
            pltpu.VMEM((HEADS, TOK), F32),
            pltpu.VMEM(shape, BF16),
        )

    spreads = (pltpu.VMEM(half, F32), pltpu.VMEM(half, F32))
    square = ((TOK, LANES), BF16)
    send, *for_mine = call(
        their_states_kernel,
        [(states, BF16), (half, BF16), (half, BF16), ((TOK, HEADS // 2), F32), square, square],
        1,
        *inputs,
        from_hbm=True,
        scratch=loaded(half) + spreads + (pltpu.SemaphoreType.DMA((7,)),),
    )
    got = lax.ppermute(send, "seq", swap)
    mine, factor = call(
        my_states_kernel,
        [((2 * TOK, HALF_WIDE), F32), ((8, HALF_WIDE), F32)],
        1,
        *for_mine,
        scratch=spreads,
    )
    (send,) = call(
        chip_kernel,
        [(slices_shape, BF16)],
        1,
        got,
        mine,
        factor,
        to_hbm=True,
        scratch=(pltpu.VMEM(slices_shape, BF16), pltpu.SemaphoreType.DMA((PAIRS // 2,))),
    )
    gathered = lax.all_to_all(send, "seq", 0, 0, tiled=True, axis_index_groups=same_core)
    local = call(
        intra_kernel,
        [
            (wide, F32),
            ((HEADS, TOK), F32),
            ((2, TOK, LANES), F32),
            (wide, BF16),
            (wide, BF16),
            ((2, TOK, LANES), BF16),
            (wide, F32),
        ],
        3,
        *inputs,
        from_hbm=True,
        scratch=loaded(wide) + (pltpu.SemaphoreType.DMA((5,)),),
    )
    gathered, (gx, inner, bc, wx, wg, mats, end) = lax.optimization_barrier((gathered, local))
    (back,) = call(functools.partial(recurrence_kernel, place), [(slices_shape, BF16)], 1, gathered)
    back = lax.all_to_all(back, "seq", 0, 0, tiled=True, axis_index_groups=same_core)
    (send,) = call(their_block_kernel, [(states, BF16)], 1, back, got, mine, factor)
    other = lax.ppermute(send, "seq", swap)
    own, part = call(
        my_block_kernel,
        [(states, BF16), ((2, TOK, LANES), F32)],
        1, back, got, mine, factor, wx, wg, bc,
    )
    (parts,) = call(
        sums_kernel,
        [((heads, 2 * TOK, LANES), BF16)],
        1,
        other,
        wx,
        wg,
        part,
        to_hbm=True,
        scratch=(pltpu.VMEM((2 * TOK, LANES), BF16), pltpu.SemaphoreType.DMA((2, heads))),
    )
    parts = lax.all_to_all(parts, "head", 0, 0, tiled=True, axis_index_groups=planes)
    grad_x, decay_grad = call(
        grads_kernel,
        [(wide, BF16), ((HEADS, TOK), F32)],
        3,
        own, other, wx, wg, mats, gx, inner, end,
    )
    parts, grad_x, decay_grad = lax.optimization_barrier((parts, grad_x, decay_grad))
    grad_b, grad_c = call(head_sum_kernel, [((TOK, LANES), BF16)] * 2, 1, parts)
    return grad_x, grad_b, grad_c, decay_grad


def solution(mesh):
    in_specs = (
        P("seq", "head"),
        P("seq", None),
        P("seq", None),
        P("head", "seq"),
        P("seq", "head"),
    )
    out_specs = (P("seq", "head"), P("seq", None), P("seq", None), P("head", "seq"))
    return jax.shard_map(
        functools.partial(per_device, mesh.shape["seq"], mesh.shape["head"]),
        mesh=mesh,
        in_specs=in_specs,
        out_specs=out_specs,
        check_vma=False,
    )
```
